128 devices in a mesh: rows: 32 (over z, y, core), cols: 4 (over x).
Axes of the slice: x: 4, y: 4, z: 4, core: 2. Of those that a mesh axis runs over, the one named last changes fastest.
Arguments:
- coupling: float32 [1024, 4, 2, 128, 128], P('rows', 'cols'), may hold values from 1.9 to 2120
- coupling_index: int32 [1024, 4, 2], P('rows', 'cols'), may hold values from 0 to 31, as said below
- near_cost: float32 [1024, 3, 128, 128], P('rows'), may hold values from 0 to 2
- near_index: int32 [1024, 3], P('rows'), may hold values from 0 to 1023, as said below
- source_weights: int32 [131072], P('rows'), may hold values from 1 to 98
- target_cost: float32 [4, 32, 3, 128, 128], P('cols', 'rows'), may hold values from 0 to 2
- target_index: int32 [4, 32, 3], P('cols'), may hold values from 0 to 31, as said below
- target_weights: int32 [4, 4096], P('cols', 'rows'), may hold values from 1 to 98
Outputs:
- cost_blocks: float32 [1024, 4, 2, 128, 128], P('rows', 'cols')
- source_potential: float32 [131072], P('rows')
- target_potential: float32 [4, 4096], P('cols', 'rows')
The draws below stay inside these ranges and needn't reach their ends.
Inputs may be any that keep to these rules, and one draw needn't show every extreme that they name: `coupling_index`: the 2 entries of one block row and group differ; every target block of every group is named by some block row. near_index[i, 0] = i; the 3 entries of a row differ and lie in the same aligned group of 4 block rows as i. target_index[c, j, 0] = j; the 3 entries of a row differ.
All inputs are finite; a program needn't handle non-finite values.
Results may differ from the reference program's by a relative error of at most 0.0003.
Values sent between devices are 32-bit elements; how exact they have to be, the bound alone decides.
A program may use at most 256 MiB of HBM per device.

```python
import jax
import jax.numpy as jnp
from jax import lax

BLK = 128
KC1 = 3
KC2 = 3
KPC = 2
SUB = 4
ITERS = 3
GROUPS = 4
KP = 8
NB = 1024
NS = 131072
GB = 32
NT = 16384


def draw_coupling(key, part):
    key = jax.random.fold_in(key, 6)
    shape = (NB, GROUPS, KPC, BLK, BLK)
    spread = jax.random.truncated_normal(key, -3.5, 3.5, shape, jnp.float32)
    return 64.0 * jnp.exp(spread)


def draw_coupling_index(key, part):
    key = jax.random.fold_in(key, 1)
    first_key, second_key = jax.random.split(key)
    block_rows = jnp.arange(NB, dtype=jnp.int32)
    anchors = jax.random.randint(first_key, (NB // SUB, GROUPS), 0, GB, dtype=jnp.int32)[block_rows // SUB]
    jitter = jax.random.randint(second_key, (NB, GROUPS), 0, 2, dtype=jnp.int32)
    second = jnp.broadcast_to((block_rows % GB)[:, None], (NB, GROUPS))
    first = (anchors + jitter) % GB
    first = jnp.where(first == second, (first + 1) % GB, first)
    return jnp.stack([first, second], axis=-1)


def draw_near_index(key, part):
    key = jax.random.fold_in(key, 2)
    first_key, second_key = jax.random.split(key)
    block_rows = jnp.arange(NB, dtype=jnp.int32)
    inside = block_rows % SUB
    start = block_rows - inside
    offset_one = jax.random.randint(first_key, (NB,), 1, SUB, dtype=jnp.int32)
    turn = jax.random.randint(second_key, (NB,), 0, SUB - 2, dtype=jnp.int32)
    offset_two = (offset_one + turn) % (SUB - 1) + 1
    return jnp.stack([block_rows, start + (inside + offset_one) % SUB, start + (inside + offset_two) % SUB], axis=-1)


def draw_target_index(key, part):
    key = jax.random.fold_in(key, 3)
    first_key, second_key = jax.random.split(key)
    target_rows = jnp.broadcast_to(jnp.arange(GB, dtype=jnp.int32)[None, :], (GROUPS, GB))
    ahead = jax.random.randint(first_key, (GROUPS, GB), 1, 3, dtype=jnp.int32)
    behind = jax.random.randint(second_key, (GROUPS, GB), 1, 3, dtype=jnp.int32)
    return jnp.stack([target_rows, (target_rows + ahead) % GB, (target_rows + GB - behind) % GB], axis=-1)


def draw_source_weights(key, part):
    key = jax.random.fold_in(key, 4)
    places = jnp.arange(NS, dtype=jnp.int32)
    upper = 34 + 66 * places // NS
    return jax.random.randint(key, (NS,), 1, upper, dtype=jnp.int32)


def draw_target_weights(key, part):
    key = jax.random.fold_in(key, 5)
    places = jnp.arange(NT, dtype=jnp.int32)
    upper = 34 + 66 * places // NT
    return jax.random.randint(key, (NT,), 1, upper, dtype=jnp.int32).reshape(GROUPS, GB * BLK)


def block_scale(own_key, dims, shards, smallest, top_value):
    def one(axis_at, shards_of):
        draws = jax.random.uniform(jax.random.fold_in(jax.random.fold_in(own_key, 6), axis_at), (shards_of,), jnp.float32, smallest / len(shards), top_value / len(shards))
        return jnp.repeat(jnp.exp(draws), dims[axis_at] // shards_of).reshape((-1,) + (1,) * (len(dims) - axis_at - 1))

    level = one(*shards[0])
    for cut in shards[1:]:
        level = level * one(*cut)
    return level


def setup_inputs(seed: int = 0) -> dict:
    key_of = jax.random.split(jax.random.key(seed), 9)
    return {
        "coupling": draw_coupling(jax.random.fold_in(key_of[8], 71), 0),
        "coupling_index": draw_coupling_index(jax.random.fold_in(key_of[8], 71), 0),
        "near_cost": jnp.clip(2.0 * jax.random.uniform(key_of[2], (NB, KC1, BLK, BLK), jnp.float32) ** block_scale(key_of[2], (NB, KC1, BLK, BLK), ((0, 32),), -0.2, 0.2), 0.0, 2.0),
        "near_index": draw_near_index(jax.random.fold_in(key_of[8], 71), 0),
        "source_weights": draw_source_weights(jax.random.fold_in(key_of[8], 71), 0),
        "target_cost": jnp.clip(2.0 * jax.random.uniform(key_of[5], (GROUPS, GB, KC2, BLK, BLK), jnp.float32) ** block_scale(key_of[5], (GROUPS, GB, KC2, BLK, BLK), ((0, 4), (1, 32)), -0.2, 0.2), 0.0, 2.0),
        "target_index": draw_target_index(jax.random.fold_in(key_of[8], 71), 0),
        "target_weights": draw_target_weights(jax.random.fold_in(key_of[8], 71), 0),
    }


entropy = 0.01
full_precision = lax.Precision.HIGHEST


def reference(coupling, coupling_index, near_cost, near_index, source_weights, target_cost, target_index, target_weights):
    source_float = source_weights.astype(jnp.float32)
    source_mass = (NS * source_float / jnp.sum(source_float)).reshape(NB, BLK)
    target_float = target_weights.astype(jnp.float32)
    target_mass = (NT * target_float / jnp.sum(target_float)).reshape(GROUPS, GB, BLK)
    scale_near = 1.0 / (KC1 * BLK)
    scale_far = 1.0 / (KP * BLK)
    row_term = jnp.einsum("ikxy,iky->ix", near_cost * near_cost, source_mass[near_index], precision=full_precision) * scale_near
    spread_terms = jnp.einsum("cjw,cjmwz->cjmz", target_mass, target_cost * target_cost, precision=full_precision)
    one_hot = (target_index[..., None] == jnp.arange(GB)[None, None, None, :]).astype(jnp.float32)
    column_term = jnp.einsum("cjmz,cjmt->ctz", spread_terms, one_hot, precision=full_precision) / (KC2 * BLK)
    group_ids = jnp.arange(GROUPS)[None, :, None]

    def one_row(row_args):
        row_cost, row_near, row_slots = row_args
        far_plan = coupling[row_near]
        partial_blocks = jnp.einsum("kxy,kcqyz->kcqxz", row_cost, far_plan, precision=full_precision)
        far_slots = coupling_index[row_near]
        far_blocks = target_cost[group_ids, far_slots]
        through = jnp.einsum("kcqxy,kcqmyz->kcqmxz", partial_blocks, far_blocks, precision=full_precision)
        landing = target_index[group_ids, far_slots]
        match = (landing[..., None] == row_slots[None, :, None, None, :]).astype(jnp.float32)
        return jnp.einsum("kcqmxz,kcqml->clxz", through, match, precision=full_precision)

    product = lax.map(one_row, (near_cost, near_index, coupling_index))
    column_slots = column_term[group_ids, coupling_index]
    cost_blocks = row_term[:, None, None, :, None] + column_slots[:, :, :, None, :] - 2.0 * scale_near * scale_far * product
    log_source = jnp.log(source_mass)
    log_target = jnp.log(target_mass).reshape(GROUPS * GB, BLK)
    segment_ids = (group_ids * GB + coupling_index).reshape(-1)
    target_potential = jnp.zeros((GROUPS, GB, BLK), jnp.float32)
    source_potential = jnp.zeros((NB, BLK), jnp.float32)
    for step in range(ITERS):
        gathered = target_potential[group_ids, coupling_index]
        scores = (gathered[:, :, :, None, :] - cost_blocks) / entropy
        row_peak = jnp.max(scores, axis=(1, 2, 4))
        row_total = jnp.sum(jnp.exp(scores - row_peak[:, None, None, :, None]), axis=(1, 2, 4))
        source_potential = entropy * (log_source - (row_peak + jnp.log(row_total)))
        back_scores = (source_potential[:, None, None, :, None] - cost_blocks) / entropy
        slot_peak = jnp.max(back_scores, axis=3).reshape(-1, BLK)
        column_peak = jax.ops.segment_max(slot_peak, segment_ids, num_segments=GROUPS * GB)
        shifted = back_scores - column_peak[segment_ids].reshape(NB, GROUPS, KPC, 1, BLK)
        slot_total = jnp.sum(jnp.exp(shifted), axis=3).reshape(-1, BLK)
        column_total = jax.ops.segment_sum(slot_total, segment_ids, num_segments=GROUPS * GB)
        target_potential = (entropy * (log_target - (column_peak + jnp.log(column_total)))).reshape(GROUPS, GB, BLK)
    return cost_blocks, source_potential.reshape(NS), target_potential.reshape(GROUPS, GB * BLK)
```

```python
import functools

import jax
import jax.numpy as jnp
from jax import lax
from jax.experimental import pallas as pl
from jax.experimental.pallas import tpu as pltpu
from jax.sharding import PartitionSpec as P

MESH = pl.DeviceIdType.MESH
BLK = 128
ROWS = 32
NEAR = 3
LINKS = 3
SLOTS = 2
GB = 32
ITERS = 3
SHARD = LINKS * BLK
HALF = SHARD // 2
QUARTER = SHARD // 4
COLS = 4
ENTROPY = 0.01
LOW = -1e30
f32 = jnp.float32
bf16 = jnp.bfloat16


def gather_plan():
    pieces = []
    for dz in range(4):
        for dy in range(4):
            if dz == 0 and dy == 0:
                continue
            for half in range(2):
                low = half * HALF
                if half == 0:
                    axis = "z" if dz else "y"
                else:
                    axis = "y" if dy else "z"
                far = dz if axis == "z" else dy
                if far == 1:
                    cuts = [(1, low, HALF)]
                elif far == 3:
                    cuts = [(-1, low, HALF)]
                else:
                    cuts = [(-1, low, QUARTER), (1, low + QUARTER, QUARTER)]
                hops = min(dz, 4 - dz) + min(dy, 4 - dy)
                for side, first, size in cuts:
                    pieces.append((hops, half, dz, dy, first, size, axis, side))
    pieces.sort(key=lambda p: (p[0], p[2] != 0 if p[1] == 0 else p[3] != 0, p[5] != HALF, p[2], p[3], p[1]))
    return pieces


PIECES = gather_plan()


def split(value):
    high = value.astype(bf16)
    return high, (value - high.astype(f32)).astype(bf16)


def dot(a, b):
    return jnp.dot(a, b, preferred_element_type=f32)


def kernel(
    slots,
    near,
    links,
    source_ref,
    weight_ref,
    coupling_hbm,
    near_hbm,
    target_hbm,
    cost_hbm,
    source_out,
    target_out,
    near_cost,
    plan,
    plan_high,
    plan_low,
    partial,
    row_sum,
    gathered,
    far_high,
    far_low,
    cost,
    scaled,
    source_float,
    source_rows,
    weight_float,
    weight_land,
    extra,
    column,
    log_source,
    log_target,
    row_lse,
    row_land,
    source_pot,
    half_out,
    half_land,
    merged,
    merged_land,
    target_pot,
    peaks,
    sums,
    load_sem,
    gather_send,
    gather_recv,
    pair_send,
    pair_recv,
    early_send,
    early_recv,
    extra_send,
    extra_recv,
    row_send,
    row_recv,
    half_send,
    half_recv,
    merge_send,
    merge_recv,
    pot_send,
    pot_recv,
):
    rank = lax.axis_index("rows")
    group = lax.axis_index("cols")
    z = rank // 8
    y = (rank // 2) % 4
    core = rank % 2

    def at(dz, dy, other=0):
        return (((z + dz) % 4) * 4 + (y + dy) % 4) * 2 + (core + other) % 2

    def device(dz, dy, other=0, dx=0):
        return (at(dz, dy, other), (group + dx) % COLS)

    def remote(src, dst, send, recv, where):
        return pltpu.make_async_remote_copy(
            src_ref=src, dst_ref=dst, send_sem=send, recv_sem=recv, device_id=where, device_id_type=MESH
        )

    def shard_rows(dz, dy, first, size, other=0):
        return gathered.at[pl.ds(pl.multiple_of(at(dz, dy, other) * SHARD + first, 8), size)]

    loads = []
    chunk = ROWS // 4
    for part in range(4):
        loads.append(
            pltpu.make_async_copy(
                coupling_hbm.at[pl.ds(part * chunk * SLOTS, chunk * SLOTS)],
                plan.at[pl.ds(part * chunk * SLOTS, chunk * SLOTS)],
                load_sem.at[part],
            )
        )
    for part in range(4):
        loads.append(
            pltpu.make_async_copy(
                near_hbm.at[pl.ds(part * chunk * NEAR, chunk * NEAR)],
                near_cost.at[pl.ds(part * chunk * NEAR, chunk * NEAR)],
                load_sem.at[4 + part],
            )
        )
    own_rows = gathered.at[pl.ds(pl.multiple_of(rank * SHARD, 8), SHARD)]
    own_load = pltpu.make_async_copy(target_hbm, own_rows, load_sem.at[8])
    own_load.start()

    barrier = pltpu.get_barrier_semaphore()
    neighbours = [device(0, 0, 1), device(0, 1), device(0, 3), device(1, 0), device(3, 0)]
    neighbours += [device(0, 0, 0, dx) for dx in (1, 2, 3)]
    for where in neighbours:
        pl.semaphore_signal(barrier, inc=1, device_id=where, device_id_type=MESH)
    weight_float[...] = weight_ref[...].astype(f32)
    source_float[...] = source_ref[...].astype(f32)
    source_rows[...] = source_float[...].reshape(ROWS, 1, BLK)
    pl.semaphore_wait(barrier, len(neighbours))

    started = []

    def start(copy):
        copy.start()
        started.append(copy)

    held = set()
    sent = set()

    def send_ready():
        for number, (hops, half, dz, dy, first, size, axis, side) in enumerate(PIECES):
            if number in sent:
                continue
            from_z, from_y = (((dz - side) % 4), dy) if axis == "z" else (dz, ((dy - side) % 4))
            if from_z == 0 and from_y == 0:
                src = target_hbm.at[pl.ds(first, size)]
            else:
                covered = sum(
                    p[5]
                    for n, p in enumerate(PIECES)
                    if n in held
                    and (p[2], p[3]) == (from_z, from_y)
                    and p[4] < first + size
                    and first < p[4] + p[5]
                )
                if covered < size:
                    continue
                src = shard_rows(from_z, from_y, first, size)
            dst = shard_rows(from_z, from_y, first, size)
            where = device(-side, 0) if axis == "z" else device(0, -side)
            start(remote(src, dst, gather_send.at[number], gather_recv.at[number], where))
            sent.add(number)

    def take(number):
        hops, half, dz, dy, first, size, axis, side = PIECES[number]
        here = shard_rows(dz, dy, first, size)
        remote(here, here, gather_send.at[number], gather_recv.at[number], device(0, 0, 1)).wait_recv()
        held.add(number)
        send_ready()
        start(remote(here, here, pair_send.at[number], pair_recv.at[number], device(0, 0, 1)))

    def take_level(hops):
        for number, piece in enumerate(PIECES):
            if piece[0] == hops:
                take(number)

    send_ready()
    pair_own = len(PIECES)
    start(remote(target_hbm, own_rows, pair_send.at[pair_own], pair_recv.at[pair_own], device(0, 0, 1)))
    for copy in loads:
        copy.start()
    for dx in (1, 2, 3):
        start(
            remote(weight_float, weight_land.at[dx], early_send.at[dx], early_recv.at[dx], device(0, 0, 0, dx))
        )

    def slot_at(row, slot):
        wanted = slots[slot, row]
        return lax.rem(wanted, 2) * 16 + lax.div(wanted, 2)

    def block_at(far, wanted):
        found = jnp.int32(GB * LINKS)
        for link in range(LINKS):
            found = jnp.where(links[link, 0, far] == wanted, far * LINKS + link, found)
        return found

    def split_plan(row, _):
        for q in range(SLOTS):
            high, low = split(plan[row * SLOTS + q])
            plan_high[row, :, q * BLK : (q + 1) * BLK] = high
            plan_low[row, :, q * BLK : (q + 1) * BLK] = low
        return 0

    def first_product(row, _):
        total = jnp.zeros((BLK, BLK), f32)
        for k in range(NEAR):
            other = lax.rem(near[k, row], ROWS)
            block = near_cost[row * NEAR + k]
            high, low = split(block)
            high_plan = plan_high[other]
            low_plan = plan_low[other]
            both = jnp.concatenate([high, low], axis=1)
            result = dot(both, jnp.concatenate([high_plan, high_plan], axis=0)) + dot(high, low_plan)
            result_high, result_low = split(result)
            partial[row, 0:BLK, k * 2 * BLK : (k + 1) * 2 * BLK] = result_high
            partial[row, BLK : 2 * BLK, k * 2 * BLK : (k + 1) * 2 * BLK] = result_low
            total = total + block * block * source_rows[other]
        row_sum[row] = jnp.broadcast_to(jnp.sum(total, axis=1, keepdims=True), (BLK, BLK))
        return 0

    def first_rows(low, high):
        for part in range(4):
            if low <= part * chunk < high:
                loads[4 + part].wait()
        lax.fori_loop(low, high, first_product, 0)

    for part in range(4):
        loads[part].wait()
        lax.fori_loop(part * chunk, (part + 1) * chunk, split_plan, 0)
    first_rows(0, 4)
    take_level(1)

    own_load.wait()
    own_weight = weight_float[...]
    weight_column = jnp.broadcast_to(own_weight, (BLK, BLK)).T
    extra_rows = [own_weight]
    for link in range(LINKS):
        block = gathered[pl.ds(pl.multiple_of(rank * SHARD + link * BLK, 8), BLK), :]
        extra_rows.append(jnp.sum(block * block * weight_column, axis=0, keepdims=True))
    across = own_weight
    for dx in (1, 2, 3):
        remote(
            weight_float, weight_land.at[dx], early_send.at[dx], early_recv.at[dx], device(0, 0, 0, dx)
        ).wait_recv()
        across = across + weight_land[dx]
    extra_rows.append(across)
    extra_rows.append(jnp.sum(source_float[...], axis=0, keepdims=True))
    extra_rows.append(jnp.zeros((2, BLK), f32))
    extra[core, z, y] = jnp.concatenate(extra_rows, axis=0)

    first_rows(4, 12)
    take_level(2)
    own_extra = extra.at[core, z, y]
    for dy in (1, 2, 3):
        start(remote(own_extra, own_extra, extra_send.at[dy], extra_recv.at[dy], device(0, dy)))
    first_rows(12, 24)
    for dy in (1, 2, 3):
        remote(own_extra, own_extra, extra_send.at[dy], extra_recv.at[dy], device(0, dy)).wait_recv()
    own_extra = extra.at[core, z]
    for dz in (1, 2, 3):
        start(remote(own_extra, own_extra, extra_send.at[3 + dz], extra_recv.at[3 + dz], device(dz, 0)))
    take_level(3)
    first_rows(24, 32)
    for dz in (1, 2, 3):
        remote(own_extra, own_extra, extra_send.at[3 + dz], extra_recv.at[3 + dz], device(dz, 0)).wait_recv()
    own_extra = extra.at[core]
    start(remote(own_extra, own_extra, extra_send.at[0], extra_recv.at[0], device(0, 0, 1)))
    take_level(4)

    for number, piece in enumerate(PIECES):
        here = shard_rows(piece[2], piece[3], piece[4], piece[5], 1)
        remote(here, here, pair_send.at[number], pair_recv.at[number], device(0, 0, 1)).wait_recv()
    here = shard_rows(0, 0, 0, SHARD, 1)
    remote(here, here, pair_send.at[pair_own], pair_recv.at[pair_own], device(0, 0, 1)).wait_recv()
    remote(own_extra, own_extra, extra_send.at[0], extra_recv.at[0], device(0, 0, 1)).wait_recv()

    def split_far(step, _):
        rows = pl.multiple_of(step * SHARD, SHARD)
        for link in range(LINKS):
            high, low = split(gathered[pl.ds(rows + link * BLK, BLK), :])
            far_high[step * LINKS + link] = high
            far_low[step * LINKS + link] = low
        return 0

    lax.fori_loop(0, GB, split_far, 0)
    far_high[GB * LINKS] = jnp.zeros((BLK, BLK), bf16)
    far_low[GB * LINKS] = jnp.zeros((BLK, BLK), bf16)

    everything = extra[...].reshape(GB, 8, BLK)
    target_total = jnp.sum(everything[:, 4, :])
    source_total = jnp.sum(everything[:, 5, :])
    target_scale = (COLS * GB * BLK) / target_total
    source_scale = (GB * ROWS * BLK) / source_total
    log_source[...] = jnp.log(source_float[...] * source_scale)
    log_target[...] = jnp.log(everything[:, 0, :] * target_scale)
    column_scale = target_scale / (LINKS * BLK)
    row_scale = source_scale / (NEAR * BLK)
    position = lax.broadcasted_iota(jnp.int32, (GB, BLK), 0)

    def add_column(step, total):
        own = (step % 16) * 2 + step // 16
        for link in range(LINKS):
            lands = links[link, 0, own]
            lands = lax.rem(lands, 2) * 16 + lax.div(lands, 2)
            value = extra[step // 16, (step // 4) % 4, step % 4, 1 + link : 2 + link, :]
            total = total + jnp.where(position == lands, value, 0.0)
        return total

    column_term = lax.fori_loop(0, GB, add_column, jnp.zeros((GB, BLK), f32)) * column_scale
    column[...] = column_term.reshape(GB, 1, BLK)

    factor = 2.0 / (NEAR * BLK) / (COLS * SLOTS * BLK)

    def second_product(row, _):
        high_rows = []
        low_rows = []
        wanted = [slots[slot, row] for slot in range(SLOTS)]
        for k in range(NEAR):
            other = lax.rem(near[k, row], ROWS)
            for q in range(SLOTS):
                far = slots[q, other]
                found = [block_at(far, wanted[slot]) for slot in range(SLOTS)]
                high_rows.append(jnp.concatenate([far_high[n] for n in found], axis=1))
                low_rows.append(jnp.concatenate([far_low[n] for n in found], axis=1))
        result = dot(partial[row], jnp.concatenate(high_rows, axis=0))
        result = result[0:BLK] + result[BLK : 2 * BLK]
        result = result + dot(partial[row, 0:BLK, :], jnp.concatenate(low_rows, axis=0))
        across = row_sum[row] * row_scale
        for slot in range(SLOTS):
            own_column = column[slot_at(row, slot)]
            value = across + own_column - factor * result[:, slot * BLK : (slot + 1) * BLK]
            cost[row * SLOTS + slot] = value
            scaled[row * SLOTS + slot] = value * (1.0 / ENTROPY)
        return 0

    lax.fori_loop(0, ROWS, second_product, 0)
    out_copy = pltpu.make_async_copy(cost, cost_hbm, load_sem.at[9])
    out_copy.start()

    target_pot[0] = jnp.zeros((GB, 1, BLK), f32)
    mine = core * 16
    theirs = 16 - mine

    def row_pass(step):
        def body(part, _):
            tops = []
            totals = []
            for inner in range(8):
                row = part * 8 + inner
                scores = []
                for slot in range(SLOTS):
                    potential = target_pot[step, slot_at(row, slot)]
                    scores.append(potential - scaled[row * SLOTS + slot])
                top = jnp.max(jnp.maximum(scores[0], scores[1]), axis=1, keepdims=True)
                total = jnp.sum(jnp.exp(scores[0] - top) + jnp.exp(scores[1] - top), axis=1, keepdims=True)
                tops.append(top)
                totals.append(total)
            tops = jnp.concatenate(tops, axis=1).T
            totals = jnp.concatenate(totals, axis=1).T
            row_lse[step, pl.ds(pl.multiple_of(part * 8, 8), 8), :] = tops + jnp.log(totals)
            return 0

        lax.fori_loop(0, ROWS // 8, body, 0)

    def column_pass():
        def body(part, best):
            potentials = source_pot[pl.ds(pl.multiple_of(part * 8, 8), 8), :].T
            for inner in range(8):
                row = part * 8 + inner
                potential = potentials[:, inner : inner + 1]
                for slot in range(SLOTS):
                    block = row * SLOTS + slot
                    scores = potential - scaled[block]
                    top = jnp.max(scores, axis=0, keepdims=True)
                    total = jnp.sum(jnp.exp(scores - top), axis=0, keepdims=True)
                    peaks[pl.ds(block, 1), :] = top
                    sums[pl.ds(block, 1), :] = total
                    best = jnp.where(position == slot_at(row, slot), jnp.maximum(best, top), best)
            return best

        best = lax.fori_loop(0, ROWS // 8, body, jnp.full((GB, BLK), LOW, f32))

        def add(row, total):
            for slot in range(SLOTS):
                block = row * SLOTS + slot
                value = sums[pl.ds(block, 1), :] * jnp.exp(jnp.minimum(peaks[pl.ds(block, 1), :] - best, 0.0))
                total = total + jnp.where(position == slot_at(row, slot), value, 0.0)
            return total

        total = lax.fori_loop(0, ROWS, add, jnp.zeros((GB, BLK), f32))
        return jnp.where(total > 0.0, best + jnp.log(jnp.maximum(total, 1e-30)), LOW)

    def merge(values):
        top = functools.reduce(jnp.maximum, values)
        total = functools.reduce(jnp.add, [jnp.exp(value - top) for value in values])
        return top + jnp.log(total)

    def iteration(step):
        row_pass(step)
        copies = []
        for dx in (1, 2, 3):
            copies.append(
                remote(
                    row_lse.at[step],
                    row_land.at[step, dx - 1],
                    row_send.at[step, dx],
                    row_recv.at[step, dx],
                    device(0, 0, 0, dx),
                )
            )
            start(copies[-1])
        for copy in copies:
            copy.wait_recv()
        source_pot[...] = log_source[...] - merge([row_lse[step]] + [row_land[step, n] for n in range(3)])
        half_out[step] = column_pass()
        copy = remote(
            half_out.at[step, pl.ds(pl.multiple_of(theirs, 16), 16)],
            half_land.at[step],
            half_send.at[step],
            half_recv.at[step],
            device(0, 0, 1),
        )
        start(copy)
        copy.wait_recv()
        own = half_out[step, pl.ds(pl.multiple_of(mine, 16), 16), :]
        merged[step] = merge([own, half_land[step]])
        copies = []
        for dz in range(4):
            for dy in range(4):
                number = dz * 4 + dy
                if number:
                    copies.append(
                        remote(
                            merged.at[step],
                            merged_land.at[step, number - 1],
                            merge_send.at[step, number],
                            merge_recv.at[step, number],
                            device(dz, dy),
                        )
                    )
                    start(copies[-1])
        for copy in copies:
            copy.wait_recv()
        total = merge([merged[step]] + [merged_land[step, n] for n in range(15)])
        own = log_target[pl.ds(pl.multiple_of(mine, 16), 16), :] - total
        here = target_pot.at[step + 1, pl.ds(pl.multiple_of(mine, 16), 16)]
        here[...] = own.reshape(16, 1, BLK)
        if step < ITERS - 1:
            copy = remote(here, here, pot_send.at[step], pot_recv.at[step], device(0, 0, 1))
            start(copy)
            copy.wait_recv()

    for step in range(ITERS):
        iteration(step)
    source_out[...] = source_pot[...] * ENTROPY
    target_out[...] = target_pot[ITERS, mine + z * 4 + y] * ENTROPY
    for copy in started:
        copy.wait_send()
    out_copy.wait()


def per_device(
    coupling,
    coupling_index,
    near_cost,
    near_index,
    source_weights,
    target_cost,
    target_index,
    target_weights,
):
    smem = pl.BlockSpec(memory_space=pltpu.SMEM)
    vmem = pl.BlockSpec(memory_space=pltpu.VMEM)
    anywhere = pl.BlockSpec(memory_space=pl.ANY)
    dma = pltpu.SemaphoreType.DMA
    moves = len(PIECES)
    blocks = ROWS * SLOTS
    cost, source, target = pl.pallas_call(
        kernel,
        out_shape=(
            jax.ShapeDtypeStruct((blocks, BLK, BLK), f32),
            jax.ShapeDtypeStruct((ROWS, BLK), f32),
            jax.ShapeDtypeStruct((1, BLK), f32),
        ),
        in_specs=[smem, smem, smem, vmem, vmem, anywhere, anywhere, anywhere],
        out_specs=(anywhere, vmem, vmem),
        scratch_shapes=[
            pltpu.VMEM((ROWS * NEAR, BLK, BLK), f32),
            pltpu.VMEM((blocks, BLK, BLK), f32),
            pltpu.VMEM((ROWS, BLK, 2 * BLK), bf16),
            pltpu.VMEM((ROWS, BLK, 2 * BLK), bf16),
            pltpu.VMEM((ROWS, 2 * BLK, 6 * BLK), bf16),
            pltpu.VMEM((ROWS, BLK, BLK), f32),
            pltpu.VMEM((GB * SHARD, BLK), f32),
            pltpu.VMEM((GB * LINKS + 1, BLK, BLK), bf16),
            pltpu.VMEM((GB * LINKS + 1, BLK, BLK), bf16),
            pltpu.VMEM((blocks, BLK, BLK), f32),
            pltpu.VMEM((blocks, BLK, BLK), f32),
            pltpu.VMEM((ROWS, BLK), f32),
            pltpu.VMEM((ROWS, 1, BLK), f32),
            pltpu.VMEM((1, BLK), f32),
            pltpu.VMEM((4, 1, BLK), f32),
            pltpu.VMEM((2, 4, 4, 8, BLK), f32),
            pltpu.VMEM((GB, 1, BLK), f32),
            pltpu.VMEM((ROWS, BLK), f32),
            pltpu.VMEM((GB, BLK), f32),
            pltpu.VMEM((ITERS, ROWS, BLK), f32),
            pltpu.VMEM((ITERS, 3, ROWS, BLK), f32),
            pltpu.VMEM((ROWS, BLK), f32),
            pltpu.VMEM((ITERS, GB, BLK), f32),
            pltpu.VMEM((ITERS, 16, BLK), f32),
            pltpu.VMEM((ITERS, 16, BLK), f32),
            pltpu.VMEM((ITERS, 15, 16, BLK), f32),
            pltpu.VMEM((ITERS + 1, GB, 1, BLK), f32),
            pltpu.VMEM((blocks, BLK), f32),
            pltpu.VMEM((blocks, BLK), f32),
            dma((10,)),
            dma((moves,)),
            dma((moves,)),
            dma((moves + 1,)),
            dma((moves + 1,)),
            dma((4,)),
            dma((4,)),
            dma((7,)),
            dma((7,)),
            dma((ITERS, 4)),
            dma((ITERS, 4)),
            dma((ITERS,)),
            dma((ITERS,)),
            dma((ITERS, 16)),
            dma((ITERS, 16)),
            dma((ITERS,)),
            dma((ITERS,)),
        ],
        compiler_params=pltpu.CompilerParams(
            collective_id=0, has_side_effects=True, vmem_limit_bytes=60 * 2**20
        ),
        name="gromov_step",
    )(
        coupling_index.transpose(1, 2, 0).reshape(SLOTS, ROWS),
        near_index.T,
        target_index.transpose(2, 0, 1),
        source_weights.reshape(ROWS, BLK),
        target_weights,
        coupling.reshape(blocks, BLK, BLK),
        near_cost.reshape(ROWS * NEAR, BLK, BLK),
        target_cost.reshape(SHARD, BLK),
    )
    return (
        cost.reshape(ROWS, 1, SLOTS, BLK, BLK),
        source.reshape(ROWS * BLK),
        target,
    )


def solution(mesh):
    placed = (
        P("rows", "cols", None, None, None),
        P("rows", "cols", None),
        P("rows", None, None, None),
        P("rows", None),
        P("rows"),
        P("cols", "rows", None, None, None),
        P("cols", None, None),
        P("cols", "rows"),
    )
    return jax.shard_map(
        per_device,
        mesh=mesh,
        in_specs=placed,
        out_specs=(P("rows", "cols", None, None, None), P("rows"), P("cols", "rows")),
        check_vma=False,
    )
```

```python
import functools
import itertools

import jax
import jax.numpy as jnp
from jax import lax
from jax.experimental import pallas as pl
from jax.experimental.pallas import tpu as pltpu
from jax.sharding import PartitionSpec as P

MESH = pl.DeviceIdType.MESH
BLK = 128
ROWS = 32
NEAR = 3
LINKS = 3
SLOTS = 2
GB = 32
ITERS = 3
SHARD = LINKS * BLK
HALF = SHARD // 2
QUARTER = SHARD // 4
COLS = 4
ENTROPY = 0.01
LOW = -1e30
f32 = jnp.float32
bf16 = jnp.bfloat16


def gather_plan():
    pieces = []
    for half, dz, dy, part in itertools.product(range(2), range(4), range(4), range(2)):
        if dz == 0 and dy == 0:
            continue
        first_axis = dy if half == 0 else dz
        last_axis = dz if half == 0 else dy
        axis = ("z" if half == 0 else "y") if last_axis else ("y" if half == 0 else "z")
        far = last_axis if last_axis else first_axis
        side = {1: 1, 3: -1, 2: 2 * part - 1}[far]
        came = ((dz - side) % 4, dy) if axis == "z" else (dz, (dy - side) % 4)
        pieces.append((half, dz, dy, part, axis, side, came))

    def onward(piece):
        half, dz, dy, part = piece[:4]
        after = [p for p in pieces if p[0] == half and p[3] == part and p[6] == (dz, dy)]
        return max([1 + onward(p) for p in after], default=0)

    hops = {p: onward(p) for p in pieces}
    have = {(half, 0, 0, part): 0 for half in range(2) for part in range(2)}
    left = list(pieces)
    sends = []
    arrivals = []
    slot = 0
    while left:
        sends.append([])
        for link in itertools.product("yz", (1, -1)):
            ready = [
                p
                for p in left
                if (p[4], p[5]) == link and have.get((p[0],) + p[6] + (p[3],), slot + 1) <= slot
            ]
            if ready:
                best = max(ready, key=lambda p: (hops[p], -have[(p[0],) + p[6] + (p[3],)], -left.index(p)))
                left.remove(best)
                sends[-1].append(best)
                have[best[:4]] = slot + 1 + DELAY
                arrivals.append(best)
        slot += 1
    arrivals.sort(key=lambda p: have[p[:4]])
    takes = [[p for p in arrivals if have[p[:4]] == when] for when in range(slot + 1 + DELAY)]
    number = {p: n for n, p in enumerate(arrivals)}
    return number, sends, takes


DELAY = 3
NUMBER, SENDS, TAKES = gather_plan()


def split(value):
    high = value.astype(bf16)
    return high, (value - high.astype(f32)).astype(bf16)


def dot(a, b):
    return jnp.dot(a, b, preferred_element_type=f32)


def kernel(
    slots_hbm,
    near_index_hbm,
    links_hbm,
    source_hbm,
    weight_hbm,
    coupling_hbm,
    near_hbm,
    target_hbm,
    cost_hbm,
    source_out,
    target_out,
    slots,
    near,
    links,
    source_ref,
    weight_ref,
    near_cost,
    plan,
    plan_high,
    plan_low,
    partial,
    row_sum,
    gathered,
    far_high,
    far_low,
    cost,
    scaled,
    source_float,
    source_rows,
    weight_float,
    weight_land,
    extra,
    column,
    log_source,
    log_target,
    row_lse,
    row_land,
    source_pot,
    half_out,
    half_land,
    merged,
    merged_land,
    target_pot,
    peaks,
    sums,
    best_rows,
    load_sem,
    gather_send,
    gather_recv,
    pair_send,
    pair_recv,
    early_send,
    early_recv,
    extra_send,
    extra_recv,
    row_send,
    row_recv,
    half_send,
    half_recv,
    merge_send,
    merge_recv,
    pot_send,
    pot_recv,
):
    rank = lax.axis_index("rows")
    group = lax.axis_index("cols")
    z = rank // 8
    y = (rank // 2) % 4
    core = rank % 2

    def at(dz, dy, other=0):
        return (((z + dz) % 4) * 4 + (y + dy) % 4) * 2 + (core + other) % 2

    def device(dz, dy, other=0, dx=0):
        return (at(dz, dy, other), (group + dx) % COLS)

    def remote(src, dst, send, recv, where):
        return pltpu.make_async_remote_copy(
            src_ref=src, dst_ref=dst, send_sem=send, recv_sem=recv, device_id=where, device_id_type=MESH
        )

    def piece_rows(dz, dy, half, part, other=0):
        first = at(dz, dy, other) * SHARD + half * HALF + part * QUARTER
        return gathered.at[pl.ds(pl.multiple_of(first, 8), QUARTER)]

    loads = []
    chunk = ROWS // 4
    for part in range(4):
        loads.append(
            pltpu.make_async_copy(
                coupling_hbm.at[pl.ds(part * chunk * SLOTS, chunk * SLOTS)],
                plan.at[pl.ds(part * chunk * SLOTS, chunk * SLOTS)],
                load_sem.at[part],
            )
        )
    for part in range(4):
        loads.append(
            pltpu.make_async_copy(
                near_hbm.at[pl.ds(part * chunk * NEAR, chunk * NEAR)],
                near_cost.at[pl.ds(part * chunk * NEAR, chunk * NEAR)],
                load_sem.at[4 + part],
            )
        )
    small = []
    for number, (src, dst) in enumerate(
        [
            (weight_hbm, weight_ref),
            (source_hbm, source_ref),
            (near_index_hbm, near),
            (slots_hbm, slots),
            (links_hbm, links),
        ]
    ):
        small.append(pltpu.make_async_copy(src, dst, load_sem.at[10 + number]))
    own_rows = gathered.at[pl.ds(pl.multiple_of(rank * SHARD, 8), SHARD)]
    own_load = pltpu.make_async_copy(target_hbm, own_rows, load_sem.at[8])

    barrier = pltpu.get_barrier_semaphore()
    neighbours = [device(0, 0, 1), device(0, 1), device(0, 3), device(1, 0), device(3, 0)]
    neighbours += [device(0, 0, 0, dx) for dx in (1, 2, 3)]
    for where in neighbours:
        pl.semaphore_signal(barrier, inc=1, device_id=where, device_id_type=MESH)
    for copy in small + [own_load] + loads:
        copy.start()
    small[0].wait()
    weight_float[...] = weight_ref[...].astype(f32)
    pl.semaphore_wait(barrier, len(neighbours))

    started = []

    def start(copy):
        copy.start()
        started.append(copy)

    def send(piece):
        half, dz, dy, part, axis, side, came = piece
        dst = piece_rows(*came, half, part)
        if came == (0, 0):
            src = target_hbm.at[pl.ds(half * HALF + part * QUARTER, QUARTER)]
        else:
            src = dst
        number = NUMBER[piece]
        where = device(-side, 0) if axis == "z" else device(0, -side)
        start(remote(src, dst, gather_send.at[number], gather_recv.at[number], where))

    def split_rows(owner, half, part):
        first = half * HALF + part * QUARTER
        end = first + QUARTER
        while first < end:
            link = first // BLK
            size = min(end, (link + 1) * BLK) - first
            high, low = split(gathered[pl.ds(pl.multiple_of(owner * SHARD + first, 8), size), :])
            far_high[owner * LINKS + link, first - link * BLK : first - link * BLK + size, :] = high
            far_low[owner * LINKS + link, first - link * BLK : first - link * BLK + size, :] = low
            first += size

    def pair_copy(piece, other):
        here = piece_rows(piece[1], piece[2], piece[0], piece[3], other)
        number = NUMBER[piece]
        return remote(here, here, pair_send.at[number], pair_recv.at[number], device(0, 0, 1))

    def take(slot):
        pieces = TAKES[slot] if slot < len(TAKES) else []
        for piece in pieces:
            half, dz, dy, part = piece[:4]
            here = piece_rows(dz, dy, half, part)
            number = NUMBER[piece]
            remote(here, here, gather_send.at[number], gather_recv.at[number], device(0, 0, 1)).wait_recv()
            start(pair_copy(piece, 0))
        return pieces

    def use(pieces, other):
        for piece in pieces:
            if other:
                pair_copy(piece, 1).wait_recv()
            split_rows(at(piece[1], piece[2], other), piece[0], piece[3])

    def slot_at(row, slot):
        wanted = slots[slot, row]
        return lax.rem(wanted, 2) * 16 + lax.div(wanted, 2)

    def block_at(far, wanted):
        found = jnp.int32(GB * LINKS)
        for link in range(LINKS):
            found = jnp.where(links[link, 0, far] == wanted, far * LINKS + link, found)
        return found

    def split_plan(row, _):
        for q in range(SLOTS):
            high, low = split(plan[row * SLOTS + q])
            plan_high[row, :, q * BLK : (q + 1) * BLK] = high
            plan_low[row, :, q * BLK : (q + 1) * BLK] = low
        return 0

    def first_product(pair, _):
        for row in (2 * pair, 2 * pair + 1):
            total = jnp.zeros((BLK, BLK), f32)
            for k in range(NEAR):
                other = lax.rem(near[k, row], ROWS)
                block = near_cost[row * NEAR + k]
                high, low = split(block)
                high_plan = plan_high[other]
                low_plan = plan_low[other]
                both = jnp.concatenate([high, low], axis=1)
                result = dot(both, jnp.concatenate([high_plan, high_plan], axis=0)) + dot(high, low_plan)
                result_high, result_low = split(result)
                partial[row, 0:BLK, k * 2 * BLK : (k + 1) * 2 * BLK] = result_high
                partial[row, BLK : 2 * BLK, k * 2 * BLK : (k + 1) * 2 * BLK] = result_low
                total = total + block * block * source_rows[other]
            row_sum[row] = jnp.broadcast_to(jnp.sum(total, axis=1, keepdims=True), (BLK, BLK))
        return 0

    def first_rows(low, high):
        for part in range(4):
            if low <= part * chunk < high:
                loads[4 + part].wait()
        lax.fori_loop(low // 2, high // 2, first_product, 0)

    def plan_rows(part):
        loads[part].wait()
        lax.fori_loop(part * chunk, (part + 1) * chunk, split_plan, 0)

    def own_share():
        own_load.wait()
        own_weight = weight_float[...]
        weight_column = jnp.broadcast_to(own_weight, (BLK, BLK)).T
        extra_rows = [own_weight]
        for link in range(LINKS):
            block = gathered[pl.ds(pl.multiple_of(rank * SHARD + link * BLK, 8), BLK), :]
            extra_rows.append(jnp.sum(block * block * weight_column, axis=0, keepdims=True))
        across = own_weight
        for dx in (1, 2, 3):
            early(dx).wait_recv()
            across = across + weight_land[dx]
        extra_rows.append(across)
        extra_rows.append(jnp.sum(source_float[...], axis=0, keepdims=True))
        extra_rows.append(jnp.zeros((2, BLK), f32))
        extra[core, z, y] = jnp.concatenate(extra_rows, axis=0)

    def early(dx):
        return remote(
            weight_float, weight_land.at[dx], early_send.at[dx], early_recv.at[dx], device(0, 0, 0, dx)
        )

    def extra_copy(number):
        if number == 0:
            here, where = extra.at[core], device(0, 0, 1)
        elif number < 4:
            here, where = extra.at[core, z, y], device(0, number)
        else:
            here, where = extra.at[core, z], device(number - 3, 0)
        return remote(here, here, extra_send.at[number], extra_recv.at[number], where)

    pair_own = len(NUMBER)
    from_pair = []
    rows_done = 0
    for slot in range(len(TAKES) + 2):
        taken = take(slot)
        if slot < len(SENDS):
            for piece in SENDS[slot]:
                send(piece)
        if slot == 0:
            plan_rows(0)
            plan_rows(1)
            for copy in small[1:]:
                copy.wait()
            source_float[...] = source_ref[...].astype(f32)
            source_rows[...] = source_float[...].reshape(ROWS, 1, BLK)
        elif slot == 1:
            plan_rows(2)
            plan_rows(3)
            own_rows = gathered.at[pl.ds(pl.multiple_of(rank * SHARD, 8), SHARD)]
            start(remote(target_hbm, own_rows, pair_send.at[pair_own], pair_recv.at[pair_own], device(0, 0, 1)))
            for dx in (1, 2, 3):
                start(early(dx))
        elif slot == 4:
            own_share()
            for half, part in itertools.product(range(2), range(2)):
                split_rows(rank, half, part)
        elif slot == 8:
            for number in (1, 2, 3):
                start(extra_copy(number))
        elif slot == 11:
            for number in (1, 2, 3):
                extra_copy(number).wait_recv()
            for number in (4, 5, 6):
                start(extra_copy(number))
        elif slot == 15:
            for number in (4, 5, 6):
                extra_copy(number).wait_recv()
            start(extra_copy(0))
        use(taken, 0)
        from_pair.append(taken)
        if slot >= 2:
            use(from_pair[slot - 2], 1)
        if slot >= 2 and rows_done < ROWS:
            more = min(ROWS, rows_done + 4)
            first_rows(rows_done, more)
            rows_done = more
    here = gathered.at[pl.ds(pl.multiple_of(at(0, 0, 1) * SHARD, 8), SHARD)]
    remote(here, here, pair_send.at[pair_own], pair_recv.at[pair_own], device(0, 0, 1)).wait_recv()
    for half, part in itertools.product(range(2), range(2)):
        split_rows(at(0, 0, 1), half, part)
    extra_copy(0).wait_recv()
    far_high[GB * LINKS] = jnp.zeros((BLK, BLK), bf16)
    far_low[GB * LINKS] = jnp.zeros((BLK, BLK), bf16)

    everything = extra[...].reshape(GB, 8, BLK)
    target_total = jnp.sum(everything[:, 4, :])
    source_total = jnp.sum(everything[:, 5, :])
    target_scale = (COLS * GB * BLK) / target_total
    source_scale = (GB * ROWS * BLK) / source_total
    log_source[...] = jnp.log(source_float[...] * source_scale)
    log_target[...] = jnp.log(everything[:, 0, :] * target_scale)
    column_scale = target_scale / (LINKS * BLK)
    row_scale = source_scale / (NEAR * BLK)
    position = lax.broadcasted_iota(jnp.int32, (GB, BLK), 0)

    def add_column(step, total):
        own = (step % 16) * 2 + step // 16
        for link in range(LINKS):
            lands = links[link, 0, own]
            lands = lax.rem(lands, 2) * 16 + lax.div(lands, 2)
            value = extra[step // 16, (step // 4) % 4, step % 4, 1 + link : 2 + link, :]
            total = total + jnp.where(position == lands, value, 0.0)
        return total

    column_term = lax.fori_loop(0, GB, add_column, jnp.zeros((GB, BLK), f32)) * column_scale
    column[...] = column_term.reshape(GB, 1, BLK)

    factor = 2.0 / (NEAR * BLK) / (COLS * SLOTS * BLK)

    def second_row(row):
        high_rows = []
        low_rows = []
        wanted = [slots[slot, row] for slot in range(SLOTS)]
        for k in range(NEAR):
            other = lax.rem(near[k, row], ROWS)
            for q in range(SLOTS):
                far = slots[q, other]
                found = [block_at(far, wanted[slot]) for slot in range(SLOTS)]
                high_rows.append(jnp.concatenate([far_high[n] for n in found], axis=1))
                low_rows.append(jnp.concatenate([far_low[n] for n in found], axis=1))
        result = dot(partial[row], jnp.concatenate(high_rows, axis=0))
        result = result[0:BLK] + result[BLK : 2 * BLK]
        result = result + dot(partial[row, 0:BLK, :], jnp.concatenate(low_rows, axis=0))
        across = row_sum[row] * row_scale
        scores = []
        for slot in range(SLOTS):
            own_column = column[slot_at(row, slot)]
            value = across + own_column - factor * result[:, slot * BLK : (slot + 1) * BLK]
            cost[row * SLOTS + slot] = value
            value = value * (1.0 / ENTROPY)
            scaled[row * SLOTS + slot] = value
            scores.append(-value)
        return scores

    def row_sums(scores):
        top = jnp.max(jnp.maximum(scores[0], scores[1]), axis=1, keepdims=True)
        total = jnp.sum(jnp.exp(scores[0] - top) + jnp.exp(scores[1] - top), axis=1, keepdims=True)
        return top, total

    def row_result(found):
        tops = jnp.concatenate([top for top, _ in found], axis=1).T
        totals = jnp.concatenate([total for _, total in found], axis=1).T
        return tops + jnp.log(totals)

    def second_product(part, _):
        found = [row_sums(second_row(part * 4 + inner)) for inner in range(4)]
        row_lse[0, pl.ds(pl.multiple_of(part * 4, 4), 4), :] = row_result(found)
        return 0

    lax.fori_loop(0, ROWS // 4, second_product, 0)
    out_copy = pltpu.make_async_copy(cost, cost_hbm, load_sem.at[9])
    out_copy.start()

    mine = core * 16
    theirs = 16 - mine
    part_rows = ROWS // 2

    def row_pass(step, part):
        found = []
        for row in range(part * part_rows, (part + 1) * part_rows):
            found.append(
                row_sums(
                    [
                        target_pot[step, slot_at(row, slot)] - scaled[row * SLOTS + slot]
                        for slot in range(SLOTS)
                    ]
                )
            )
        row_lse[step, part * part_rows : (part + 1) * part_rows, :] = row_result(found)

    def column_pass(part, best):
        potentials = source_pot[part * part_rows : (part + 1) * part_rows, :].T
        for inner in range(part_rows):
            row = part * part_rows + inner
            potential = potentials[:, inner : inner + 1]
            for slot in range(SLOTS):
                block = row * SLOTS + slot
                scores = potential - scaled[block]
                top = jnp.max(scores, axis=0, keepdims=True)
                total = jnp.sum(jnp.exp(scores - top), axis=0, keepdims=True)
                peaks[block : block + 1, :] = top
                sums[block : block + 1, :] = total
                best = jnp.where(position == slot_at(row, slot), jnp.maximum(best, top), best)
        return best

    def column_result(best):
        best_rows[...] = best.reshape(GB, 1, BLK)
        every = [(row, slot) for row in range(ROWS) for slot in range(SLOTS)]
        tops = jnp.concatenate([best_rows[slot_at(row, slot)] for row, slot in every], axis=0)
        values = sums[...] * jnp.exp(peaks[...] - tops)
        total = jnp.zeros((GB, BLK), f32)
        for block, (row, slot) in enumerate(every):
            total = total + jnp.where(position == slot_at(row, slot), values[block : block + 1, :], 0.0)
        return jnp.where(total > 0.0, best + jnp.log(jnp.maximum(total, 1e-30)), LOW)

    def merge(values):
        top = functools.reduce(jnp.maximum, values)
        total = functools.reduce(jnp.add, [jnp.exp(value - top) for value in values])
        return top + jnp.log(total)

    def iteration(step, _):
        moved = []

        def move(copy):
            copy.start()
            moved.append(copy)
            return copy

        row_copies = []
        for part in range(2):
            pl.when(step > 0)(functools.partial(row_pass, step, part))
            rows = pl.ds(part * part_rows, part_rows)
            row_copies.append(
                [
                    move(
                        remote(
                            row_lse.at[step, rows],
                            row_land.at[step, dx - 1, rows],
                            row_send.at[step, part, dx],
                            row_recv.at[step, part, dx],
                            device(0, 0, 0, dx),
                        )
                    )
                    for dx in (1, 2, 3)
                ]
            )
        best = jnp.full((GB, BLK), LOW, f32)
        for part in range(2):
            for copy in row_copies[part]:
                copy.wait_recv()
            rows = slice(part * part_rows, (part + 1) * part_rows)
            arrived = [row_lse[step, rows, :]] + [row_land[step, n, rows, :] for n in range(3)]
            source_pot[rows, :] = log_source[rows, :] - merge(arrived)
            best = column_pass(part, best)
        half_out[step] = column_result(best)
        move(
            remote(
                half_out.at[step, pl.ds(pl.multiple_of(theirs, 16), 16)],
                half_land.at[step],
                half_send.at[step],
                half_recv.at[step],
                device(0, 0, 1),
            )
        ).wait_recv()
        own = half_out[step, pl.ds(pl.multiple_of(mine, 16), 16), :]
        merged[step] = merge([own, half_land[step]])
        copies = []
        for number in range(1, 16):
            copies.append(
                move(
                    remote(
                        merged.at[step],
                        merged_land.at[step, number - 1],
                        merge_send.at[step, number],
                        merge_recv.at[step, number],
                        device(number // 4, number % 4),
                    )
                )
            )
        for copy in copies:
            copy.wait_recv()
        total = merge([merged[step]] + [merged_land[step, n] for n in range(15)])
        own = log_target[pl.ds(pl.multiple_of(mine, 16), 16), :] - total
        here = target_pot.at[step + 1, pl.ds(pl.multiple_of(mine, 16), 16)]
        here[...] = own.reshape(16, 1, BLK)

        @pl.when(step < ITERS - 1)
        def _():
            copy = remote(here, here, pot_send.at[step], pot_recv.at[step], device(0, 0, 1))
            copy.start()
            copy.wait_recv()
            copy.wait_send()

        for copy in moved:
            copy.wait_send()
        return 0

    lax.fori_loop(0, ITERS, iteration, 0)
    source_out[...] = source_pot[...] * ENTROPY
    target_out[...] = target_pot[ITERS, mine + z * 4 + y] * ENTROPY
    for copy in started:
        copy.wait_send()
    out_copy.wait()


def hand_over(cost, source, target, cost_out, source_out, target_out, held, load, store):
    parts = 4
    size = held.shape[0] // parts
    refs = [(cost.at[pl.ds(n * size, size)], held.at[pl.ds(n * size, size)]) for n in range(parts)]
    loads = [pltpu.make_async_copy(src, dst, load.at[n]) for n, (src, dst) in enumerate(refs)]
    for copy in loads:
        copy.start()
    source_out[...] = source[...]
    target_out[...] = target[...]
    stores = []
    for n in range(parts):
        loads[n].wait()
        dst = cost_out.at[pl.ds(n * size, size)]
        stores.append(pltpu.make_async_copy(refs[n][1], dst, store.at[n]))
        stores[-1].start()
    for copy in stores:
        copy.wait()


def per_device(
    coupling,
    coupling_index,
    near_cost,
    near_index,
    source_weights,
    target_cost,
    target_index,
    target_weights,
):
    vmem = pl.BlockSpec(memory_space=pltpu.VMEM)
    anywhere = pl.BlockSpec(memory_space=pl.ANY)
    dma = pltpu.SemaphoreType.DMA
    moves = len(NUMBER)
    blocks = ROWS * SLOTS
    cost, source, target = pl.pallas_call(
        kernel,
        out_shape=(
            jax.ShapeDtypeStruct((blocks, BLK, BLK), f32),
            jax.ShapeDtypeStruct((ROWS, BLK), f32),
            jax.ShapeDtypeStruct((1, BLK), f32),
        ),
        in_specs=[anywhere] * 8,
        out_specs=(anywhere, vmem, vmem),
        scratch_shapes=[
            pltpu.SMEM((SLOTS, ROWS), jnp.int32),
            pltpu.SMEM((NEAR, ROWS), jnp.int32),
            pltpu.SMEM((LINKS, 1, GB), jnp.int32),
            pltpu.VMEM((ROWS, BLK), jnp.int32),
            pltpu.VMEM((1, BLK), jnp.int32),
            pltpu.VMEM((ROWS * NEAR, BLK, BLK), f32),
            pltpu.VMEM((blocks, BLK, BLK), f32),
            pltpu.VMEM((ROWS, BLK, 2 * BLK), bf16),
            pltpu.VMEM((ROWS, BLK, 2 * BLK), bf16),
            pltpu.VMEM((ROWS, 2 * BLK, 6 * BLK), bf16),
            pltpu.VMEM((ROWS, BLK, BLK), f32),
            pltpu.VMEM((GB * SHARD, BLK), f32),
            pltpu.VMEM((GB * LINKS + 1, BLK, BLK), bf16),
            pltpu.VMEM((GB * LINKS + 1, BLK, BLK), bf16),
            pltpu.VMEM((blocks, BLK, BLK), f32),
            pltpu.VMEM((blocks, BLK, BLK), f32),
            pltpu.VMEM((ROWS, BLK), f32),
            pltpu.VMEM((ROWS, 1, BLK), f32),
            pltpu.VMEM((1, BLK), f32),
            pltpu.VMEM((4, 1, BLK), f32),
            pltpu.VMEM((2, 4, 4, 8, BLK), f32),
            pltpu.VMEM((GB, 1, BLK), f32),
            pltpu.VMEM((ROWS, BLK), f32),
            pltpu.VMEM((GB, BLK), f32),
            pltpu.VMEM((ITERS, ROWS, BLK), f32),
            pltpu.VMEM((ITERS, 3, ROWS, BLK), f32),
            pltpu.VMEM((ROWS, BLK), f32),
            pltpu.VMEM((ITERS, GB, BLK), f32),
            pltpu.VMEM((ITERS, 16, BLK), f32),
            pltpu.VMEM((ITERS, 16, BLK), f32),
            pltpu.VMEM((ITERS, 15, 16, BLK), f32),
            pltpu.VMEM((ITERS + 1, GB, 1, BLK), f32),
            pltpu.VMEM((blocks, BLK), f32),
            pltpu.VMEM((blocks, BLK), f32),
            pltpu.VMEM((GB, 1, BLK), f32),
            dma((15,)),
            dma((moves,)),
            dma((moves,)),
            dma((moves + 1,)),
            dma((moves + 1,)),
            dma((4,)),
            dma((4,)),
            dma((7,)),
            dma((7,)),
            dma((ITERS, 2, 4)),
            dma((ITERS, 2, 4)),
            dma((ITERS,)),
            dma((ITERS,)),
            dma((ITERS, 16)),
            dma((ITERS, 16)),
            dma((ITERS,)),
            dma((ITERS,)),
        ],
        compiler_params=pltpu.CompilerParams(
            collective_id=0, has_side_effects=True, vmem_limit_bytes=60 * 2**20
        ),
        name="gromov_step",
    )(
        coupling_index.transpose(1, 2, 0).reshape(SLOTS, ROWS),
        near_index.T,
        target_index.transpose(2, 0, 1),
        source_weights.reshape(ROWS, BLK),
        target_weights,
        coupling.reshape(blocks, BLK, BLK),
        near_cost.reshape(ROWS * NEAR, BLK, BLK),
        target_cost.reshape(SHARD, BLK),
    )
    cost, source, target = pl.pallas_call(
        hand_over,
        out_shape=tuple(jax.ShapeDtypeStruct(x.shape, x.dtype) for x in (cost, source, target)),
        in_specs=[anywhere, vmem, vmem],
        out_specs=(anywhere, vmem, vmem),
        scratch_shapes=[pltpu.VMEM((blocks, BLK, BLK), f32), dma((4,)), dma((4,))],
        compiler_params=pltpu.CompilerParams(vmem_limit_bytes=60 * 2**20),
        name="hand_over",
    )(cost, source, target)
    return (
        cost.reshape(ROWS, 1, SLOTS, BLK, BLK),
        source.reshape(ROWS * BLK),
        target,
    )


def solution(mesh):
    placed = (
        P("rows", "cols", None, None, None),
        P("rows", "cols", None),
        P("rows", None, None, None),
        P("rows", None),
        P("rows"),
        P("cols", "rows", None, None, None),
        P("cols", None, None),
        P("cols", "rows"),
    )
    return jax.shard_map(
        per_device,
        mesh=mesh,
        in_specs=placed,
        out_specs=(P("rows", "cols", None, None, None), P("rows"), P("cols", "rows")),
        check_vma=False,
    )
```

```python
import functools
import itertools

import jax
import jax.numpy as jnp
from jax import lax
from jax.experimental import pallas as pl
from jax.experimental.pallas import tpu as pltpu
from jax.sharding import PartitionSpec as P

MESH = pl.DeviceIdType.MESH
BLK = 128
ROWS = 32
NEAR = 3
LINKS = 3
SLOTS = 2
GB = 32
ITERS = 3
SHARD = LINKS * BLK
HALF = SHARD // 2
QUARTER = SHARD // 4
COLS = 4
ENTROPY = 0.01
LOW = -1e30
f32 = jnp.float32
bf16 = jnp.bfloat16


def gather_plan():
    pieces = []
    for half, dz, dy, part in itertools.product(range(2), range(4), range(4), range(2)):
        if dz == 0 and dy == 0:
            continue
        first_axis = dy if half == 0 else dz
        last_axis = dz if half == 0 else dy
        axis = ("z" if half == 0 else "y") if last_axis else ("y" if half == 0 else "z")
        far = last_axis if last_axis else first_axis
        side = {1: 1, 3: -1, 2: 2 * part - 1}[far]
        came = ((dz - side) % 4, dy) if axis == "z" else (dz, (dy - side) % 4)
        pieces.append((half, dz, dy, part, axis, side, came))

    def onward(piece):
        half, dz, dy, part = piece[:4]
        after = [p for p in pieces if p[0] == half and p[3] == part and p[6] == (dz, dy)]
        return max([1 + onward(p) for p in after], default=0)

    hops = {p: onward(p) for p in pieces}
    have = {(half, 0, 0, part): 0 for half in range(2) for part in range(2)}
    left = list(pieces)
    sends = []
    arrivals = []
    slot = 0
    while left:
        sends.append([])
        for link in itertools.product("yz", (1, -1)):
            ready = [
                p
                for p in left
                if (p[4], p[5]) == link and have.get((p[0],) + p[6] + (p[3],), slot + 1) <= slot
            ]
            if ready:
                best = max(ready, key=lambda p: (hops[p], -have[(p[0],) + p[6] + (p[3],)], -left.index(p)))
                left.remove(best)
                sends[-1].append(best)
                have[best[:4]] = slot + 1 + DELAY
                arrivals.append(best)
        slot += 1
    arrivals.sort(key=lambda p: have[p[:4]])
    takes = [[p for p in arrivals if have[p[:4]] == when] for when in range(slot + 1 + DELAY)]
    number = {p: n for n, p in enumerate(arrivals)}
    return number, sends, takes


DELAY = 3
FARTHEST_FIRST = sorted(range(1, 16), key=lambda n: abs(n // 4 - 2) + abs(n % 4 - 2))
NUMBER, SENDS, TAKES = gather_plan()


def split(value):
    high = value.astype(bf16)
    return high, (value - high.astype(f32)).astype(bf16)


def dot(a, b):
    return jnp.dot(a, b, preferred_element_type=f32)


def kernel(
    slots_hbm,
    near_index_hbm,
    links_hbm,
    source_hbm,
    weight_hbm,
    coupling_hbm,
    near_hbm,
    target_hbm,
    cost_hbm,
    source_out,
    target_out,
    slots,
    near,
    links,
    source_ref,
    weight_ref,
    near_cost,
    plan,
    plan_high,
    plan_low,
    partial,
    row_sum,
    gathered,
    far_high,
    far_low,
    source_float,
    source_rows,
    weight_float,
    weight_land,
    extra,
    column,
    log_source,
    log_target,
    row_lse,
    row_land,
    source_pot,
    half_out,
    half_land,
    merged,
    merged_land,
    target_pot,
    peaks,
    sums,
    best_rows,
    load_sem,
    gather_send,
    gather_recv,
    pair_send,
    pair_recv,
    early_send,
    early_recv,
    extra_send,
    extra_recv,
    row_send,
    row_recv,
    half_send,
    half_recv,
    merge_send,
    merge_recv,
    pot_send,
    pot_recv,
):
    cost = plan
    scaled = near_cost

    rank = lax.axis_index("rows")
    group = lax.axis_index("cols")
    z = rank // 8
    y = (rank // 2) % 4
    core = rank % 2

    def at(dz, dy, other=0):
        return (((z + dz) % 4) * 4 + (y + dy) % 4) * 2 + (core + other) % 2

    def device(dz, dy, other=0, dx=0):
        return (at(dz, dy, other), (group + dx) % COLS)

    def remote(src, dst, send, recv, where):
        return pltpu.make_async_remote_copy(
            src_ref=src, dst_ref=dst, send_sem=send, recv_sem=recv, device_id=where, device_id_type=MESH
        )

    def piece_rows(dz, dy, half, part, other=0):
        first = at(dz, dy, other) * SHARD + half * HALF + part * QUARTER
        return gathered.at[pl.ds(pl.multiple_of(first, 8), QUARTER)]

    loads = []
    chunk = ROWS // 4
    for part in range(4):
        loads.append(
            pltpu.make_async_copy(
                coupling_hbm.at[pl.ds(part * chunk * SLOTS, chunk * SLOTS)],
                plan.at[pl.ds(part * chunk * SLOTS, chunk * SLOTS)],
                load_sem.at[part],
            )
        )
    for part in range(4):
        loads.append(
            pltpu.make_async_copy(
                near_hbm.at[pl.ds(part * chunk * NEAR, chunk * NEAR)],
                near_cost.at[pl.ds(part * chunk * NEAR, chunk * NEAR)],
                load_sem.at[4 + part],
            )
        )
    small = []
    for number, (src, dst) in enumerate(
        [
            (weight_hbm, weight_ref),
            (source_hbm, source_ref),
            (near_index_hbm, near),
            (slots_hbm, slots),
            (links_hbm, links),
        ]
    ):
        small.append(pltpu.make_async_copy(src, dst, load_sem.at[10 + number]))
    own_rows = gathered.at[pl.ds(pl.multiple_of(rank * SHARD, 8), SHARD)]
    own_load = pltpu.make_async_copy(target_hbm, own_rows, load_sem.at[8])

    barrier = pltpu.get_barrier_semaphore()
    neighbours = [device(0, 0, 1), device(0, 1), device(0, 3), device(1, 0), device(3, 0)]
    neighbours += [device(0, 0, 0, dx) for dx in (1, 3)]
    for where in neighbours:
        pl.semaphore_signal(barrier, inc=1, device_id=where, device_id_type=MESH)
    for copy in small + [own_load] + loads:
        copy.start()
    small[0].wait()
    weight_float[...] = weight_ref[...].astype(f32)
    pl.semaphore_wait(barrier, len(neighbours))

    started = []

    def start(copy):
        copy.start()
        started.append(copy)

    def send(piece):
        half, dz, dy, part, axis, side, came = piece
        dst = piece_rows(*came, half, part)
        if came == (0, 0):
            src = target_hbm.at[pl.ds(half * HALF + part * QUARTER, QUARTER)]
        else:
            src = dst
        number = NUMBER[piece]
        where = device(-side, 0) if axis == "z" else device(0, -side)
        start(remote(src, dst, gather_send.at[number], gather_recv.at[number], where))

    def split_rows(owner, half, part):
        first = half * HALF + part * QUARTER
        end = first + QUARTER
        while first < end:
            link = first // BLK
            size = min(end, (link + 1) * BLK) - first
            high, low = split(gathered[pl.ds(pl.multiple_of(owner * SHARD + first, 8), size), :])
            far_high[owner * LINKS + link, first - link * BLK : first - link * BLK + size, :] = high
            far_low[owner * LINKS + link, first - link * BLK : first - link * BLK + size, :] = low
            first += size

    def pair_copy(piece, other):
        here = piece_rows(piece[1], piece[2], piece[0], piece[3], other)
        number = NUMBER[piece]
        return remote(here, here, pair_send.at[number], pair_recv.at[number], device(0, 0, 1))

    def take(slot):
        pieces = TAKES[slot] if slot < len(TAKES) else []
        for piece in pieces:
            half, dz, dy, part = piece[:4]
            here = piece_rows(dz, dy, half, part)
            number = NUMBER[piece]
            remote(here, here, gather_send.at[number], gather_recv.at[number], device(0, 0, 1)).wait_recv()
            start(pair_copy(piece, 0))
        return pieces

    def use(pieces, other):
        for piece in pieces:
            if other:
                pair_copy(piece, 1).wait_recv()
            split_rows(at(piece[1], piece[2], other), piece[0], piece[3])

    def slot_at(row, slot):
        wanted = slots[slot, row]
        return lax.rem(wanted, 2) * 16 + lax.div(wanted, 2)

    def block_at(far, wanted):
        found = jnp.int32(GB * LINKS)
        for link in range(LINKS):
            found = jnp.where(links[link, 0, far] == wanted, far * LINKS + link, found)
        return found

    def split_plan(row, _):
        for q in range(SLOTS):
            high, low = split(plan[row * SLOTS + q])
            plan_high[row, :, q * BLK : (q + 1) * BLK] = high
            plan_low[row, :, q * BLK : (q + 1) * BLK] = low
        return 0

    def first_product(pair, _):
        for row in (2 * pair, 2 * pair + 1):
            total = jnp.zeros((BLK, BLK), f32)
            for k in range(NEAR):
                other = lax.rem(near[k, row], ROWS)
                block = near_cost[row * NEAR + k]
                high, low = split(block)
                high_plan = plan_high[other]
                low_plan = plan_low[other]
                both = jnp.concatenate([high, low], axis=1)
                result = dot(both, jnp.concatenate([high_plan, high_plan], axis=0)) + dot(high, low_plan)
                result_high, result_low = split(result)
                partial[row, 0:BLK, k * 2 * BLK : (k + 1) * 2 * BLK] = result_high
                partial[row, BLK : 2 * BLK, k * 2 * BLK : (k + 1) * 2 * BLK] = result_low
                total = total + block * block * source_rows[other]
            row_sum[row] = jnp.broadcast_to(jnp.sum(total, axis=1, keepdims=True), (BLK, BLK))
        return 0

    def first_rows(low, high):
        for part in range(4):
            if low <= part * chunk < high:
                loads[4 + part].wait()
        lax.fori_loop(low // 2, high // 2, first_product, 0)

    def plan_rows(part):
        loads[part].wait()
        lax.fori_loop(part * chunk, (part + 1) * chunk, split_plan, 0)

    def own_share():
        own_load.wait()
        own_weight = weight_float[...]
        weight_column = jnp.broadcast_to(own_weight, (BLK, BLK)).T
        extra_rows = [own_weight]
        for link in range(LINKS):
            block = gathered[pl.ds(pl.multiple_of(rank * SHARD + link * BLK, 8), BLK), :]
            extra_rows.append(jnp.sum(block * block * weight_column, axis=0, keepdims=True))
        across = own_weight
        for dx in (3, 2):
            early(dx).wait_recv()
        for dx in (1, 2, 3):
            across = across + weight_land[dx]
        extra_rows.append(across)
        extra_rows.append(jnp.sum(source_float[...], axis=0, keepdims=True))
        extra_rows.append(jnp.zeros((2, BLK), f32))
        extra[core, z, y] = jnp.concatenate(extra_rows, axis=0)

    def early(dx):
        src = weight_land.at[1] if dx == 2 else weight_float
        where = device(0, 0, 0, 1 if dx == 2 else dx)
        return remote(src, weight_land.at[dx], early_send.at[dx], early_recv.at[dx], where)

    def extra_copy(number):
        if number == 0:
            here, where = extra.at[core], device(0, 0, 1)
        elif number < 4:
            here, where = extra.at[core, z, y], device(0, number)
        else:
            here, where = extra.at[core, z], device(number - 3, 0)
        return remote(here, here, extra_send.at[number], extra_recv.at[number], where)

    pair_own = len(NUMBER)
    from_pair = []
    rows_done = 0
    for slot in range(len(TAKES) + 2):
        taken = take(slot)
        if slot < len(SENDS):
            for piece in SENDS[slot]:
                send(piece)
        if slot == 0:
            plan_rows(0)
            plan_rows(1)
            for copy in small[1:]:
                copy.wait()
            source_float[...] = source_ref[...].astype(f32)
            source_rows[...] = source_float[...].reshape(ROWS, 1, BLK)
        elif slot == 1:
            plan_rows(2)
            plan_rows(3)
            own_rows = gathered.at[pl.ds(pl.multiple_of(rank * SHARD, 8), SHARD)]
            start(remote(target_hbm, own_rows, pair_send.at[pair_own], pair_recv.at[pair_own], device(0, 0, 1)))
            start(early(1))
            start(early(3))
        elif slot == 4:
            early(1).wait_recv()
            start(early(2))
        elif slot == 6:
            own_share()
            for half, part in itertools.product(range(2), range(2)):
                split_rows(rank, half, part)
        elif slot == 8:
            for number in (1, 2, 3):
                start(extra_copy(number))
        elif slot == 11:
            for number in (1, 2, 3):
                extra_copy(number).wait_recv()
            for number in (4, 5, 6):
                start(extra_copy(number))
        elif slot == 15:
            for number in (4, 5, 6):
                extra_copy(number).wait_recv()
            start(extra_copy(0))
        use(taken, 0)
        from_pair.append(taken)
        if slot >= 2:
            use(from_pair[slot - 2], 1)
        if slot >= 2 and rows_done < ROWS:
            more = min(ROWS, rows_done + 4)
            first_rows(rows_done, more)
            rows_done = more
    here = gathered.at[pl.ds(pl.multiple_of(at(0, 0, 1) * SHARD, 8), SHARD)]
    remote(here, here, pair_send.at[pair_own], pair_recv.at[pair_own], device(0, 0, 1)).wait_recv()
    for half, part in itertools.product(range(2), range(2)):
        split_rows(at(0, 0, 1), half, part)
    extra_copy(0).wait_recv()
    far_high[GB * LINKS] = jnp.zeros((BLK, BLK), bf16)
    far_low[GB * LINKS] = jnp.zeros((BLK, BLK), bf16)

    everything = extra[...].reshape(GB, 8, BLK)
    target_total = jnp.sum(everything[:, 4, :])
    source_total = jnp.sum(everything[:, 5, :])
    target_scale = (COLS * GB * BLK) / target_total
    source_scale = (GB * ROWS * BLK) / source_total
    log_source[...] = jnp.log(source_float[...] * source_scale)
    log_target[...] = jnp.log(everything[:, 0, :] * target_scale)
    column_scale = target_scale / (LINKS * BLK)
    row_scale = source_scale / (NEAR * BLK)
    position = lax.broadcasted_iota(jnp.int32, (GB, BLK), 0)

    def add_column(step, total):
        own = (step % 16) * 2 + step // 16
        for link in range(LINKS):
            lands = links[link, 0, own]
            lands = lax.rem(lands, 2) * 16 + lax.div(lands, 2)
            value = extra[step // 16, (step // 4) % 4, step % 4, 1 + link : 2 + link, :]
            total = total + jnp.where(position == lands, value, 0.0)
        return total

    column_term = lax.fori_loop(0, GB, add_column, jnp.zeros((GB, BLK), f32)) * column_scale
    column[...] = column_term.reshape(GB, 1, BLK)

    factor = 2.0 / (NEAR * BLK) / (COLS * SLOTS * BLK)

    def second_row(row):
        high_rows = []
        low_rows = []
        wanted = [slots[slot, row] for slot in range(SLOTS)]
        for k in range(NEAR):
            other = lax.rem(near[k, row], ROWS)
            for q in range(SLOTS):
                far = slots[q, other]
                found = [block_at(far, wanted[slot]) for slot in range(SLOTS)]
                high_rows.append(jnp.concatenate([far_high[n] for n in found], axis=1))
                low_rows.append(jnp.concatenate([far_low[n] for n in found], axis=1))
        result = dot(partial[row], jnp.concatenate(high_rows, axis=0))
        result = result[0:BLK] + result[BLK : 2 * BLK]
        result = result + dot(partial[row, 0:BLK, :], jnp.concatenate(low_rows, axis=0))
        across = row_sum[row] * row_scale
        scores = []
        for slot in range(SLOTS):
            own_column = column[slot_at(row, slot)]
            value = across + own_column - factor * result[:, slot * BLK : (slot + 1) * BLK]
            cost[row * SLOTS + slot] = value
            value = value * (1.0 / ENTROPY)
            scaled[row * SLOTS + slot] = value
            scores.append(-value)
        return scores

    def row_sums(scores):
        top = jnp.max(jnp.maximum(scores[0], scores[1]), axis=1, keepdims=True)
        total = jnp.sum(jnp.exp(scores[0] - top) + jnp.exp(scores[1] - top), axis=1, keepdims=True)
        return top, total

    def row_result(found):
        tops = jnp.concatenate([top for top, _ in found], axis=1).T
        totals = jnp.concatenate([total for _, total in found], axis=1).T
        return tops + jnp.log(totals)

    def second_product(part, _):
        found = [row_sums(second_row(part * 4 + inner)) for inner in range(4)]
        row_lse[0, pl.ds(pl.multiple_of(part * 4, 4), 4), :] = row_result(found)
        return 0

    lax.fori_loop(0, ROWS // 4, second_product, 0)
    out_copy = pltpu.make_async_copy(cost, cost_hbm, load_sem.at[9])
    out_copy.start()

    mine = core * 16
    theirs = 16 - mine
    part_rows = ROWS // 2

    def row_pass(step, part):
        found = []
        for row in range(part * part_rows, (part + 1) * part_rows):
            found.append(
                row_sums(
                    [
                        target_pot[step, slot_at(row, slot)] - scaled[row * SLOTS + slot]
                        for slot in range(SLOTS)
                    ]
                )
            )
        row_lse[step, part * part_rows : (part + 1) * part_rows, :] = row_result(found)

    def column_pass(part, best):
        potentials = source_pot[part * part_rows : (part + 1) * part_rows, :].T
        for inner in range(part_rows):
            row = part * part_rows + inner
            potential = potentials[:, inner : inner + 1]
            for slot in range(SLOTS):
                block = row * SLOTS + slot
                scores = potential - scaled[block]
                top = jnp.max(scores, axis=0, keepdims=True)
                total = jnp.sum(jnp.exp(scores - top), axis=0, keepdims=True)
                peaks[block : block + 1, :] = top
                sums[block : block + 1, :] = total
                best = jnp.where(position == slot_at(row, slot), jnp.maximum(best, top), best)
        return best

    def column_result(best):
        best_rows[...] = best.reshape(GB, 1, BLK)
        every = [(row, slot) for row in range(ROWS) for slot in range(SLOTS)]
        tops = jnp.concatenate([best_rows[slot_at(row, slot)] for row, slot in every], axis=0)
        values = sums[...] * jnp.exp(peaks[...] - tops)
        total = jnp.zeros((GB, BLK), f32)
        for block, (row, slot) in enumerate(every):
            total = total + jnp.where(position == slot_at(row, slot), values[block : block + 1, :], 0.0)
        return jnp.where(total > 0.0, best + jnp.log(jnp.maximum(total, 1e-30)), LOW)

    def merge(values):
        top = functools.reduce(jnp.maximum, values)
        total = functools.reduce(jnp.add, [jnp.exp(value - top) for value in values])
        return top + jnp.log(total)

    def iteration(step, _):
        moved = []

        def move(copy):
            copy.start()
            moved.append(copy)
            return copy

        row_copies = []
        for part in range(2):
            pl.when(step > 0)(functools.partial(row_pass, step, part))
            rows = pl.ds(part * part_rows, part_rows)
            row_copies.append(
                [
                    move(
                        remote(
                            row_lse.at[step, rows],
                            row_land.at[step, dx - 1, rows],
                            row_send.at[step, part, dx],
                            row_recv.at[step, part, dx],
                            device(0, 0, 0, dx),
                        )
                    )
                    for dx in (2, 1, 3)
                ]
            )
        best = jnp.full((GB, BLK), LOW, f32)
        for part in range(2):
            for copy in row_copies[part]:
                copy.wait_recv()
            rows = slice(part * part_rows, (part + 1) * part_rows)
            arrived = [row_lse[step, rows, :]] + [row_land[step, n, rows, :] for n in range(3)]
            source_pot[rows, :] = log_source[rows, :] - merge(arrived)
            best = column_pass(part, best)
        half_out[step] = column_result(best)
        move(
            remote(
                half_out.at[step, pl.ds(pl.multiple_of(theirs, 16), 16)],
                half_land.at[step],
                half_send.at[step],
                half_recv.at[step],
                device(0, 0, 1),
            )
        ).wait_recv()
        own = half_out[step, pl.ds(pl.multiple_of(mine, 16), 16), :]
        merged[step] = merge([own, half_land[step]])
        copies = []
        for number in FARTHEST_FIRST:
            copies.append(
                move(
                    remote(
                        merged.at[step],
                        merged_land.at[step, number - 1],
                        merge_send.at[step, number],
                        merge_recv.at[step, number],
                        device(number // 4, number % 4),
                    )
                )
            )
        for copy in copies:
            copy.wait_recv()
        total = merge([merged[step]] + [merged_land[step, n] for n in range(15)])
        own = log_target[pl.ds(pl.multiple_of(mine, 16), 16), :] - total
        here = target_pot.at[step + 1, pl.ds(pl.multiple_of(mine, 16), 16)]
        here[...] = own.reshape(16, 1, BLK)

        @pl.when(step < ITERS - 1)
        def _():
            copy = remote(here, here, pot_send.at[step], pot_recv.at[step], device(0, 0, 1))
            copy.start()
            copy.wait_recv()
            copy.wait_send()

        for copy in moved:
            copy.wait_send()
        return 0

    lax.fori_loop(0, ITERS, iteration, 0)
    source_out[...] = source_pot[...] * ENTROPY
    target_out[...] = target_pot[ITERS, mine + z * 4 + y] * ENTROPY
    for copy in started:
        copy.wait_send()
    out_copy.wait()


def hand_over(cost, source, target, cost_out, source_out, target_out, held, source_held, target_held, load, store):
    parts = 4
    size = held.shape[0] // parts
    rows = [pl.ds(n * size, size) for n in range(parts)]
    steps = [(cost.at[r], held.at[r], cost_out.at[r]) for r in rows]
    steps[1:1] = [(source, source_held, source_out), (target, target_held, target_out)]
    loads = [pltpu.make_async_copy(src, here, load.at[n]) for n, (src, here, _) in enumerate(steps)]
    stores = [pltpu.make_async_copy(here, dst, store.at[n]) for n, (_, here, dst) in enumerate(steps)]
    for copy in loads:
        copy.start()
    for came, goes in zip(loads, stores):
        came.wait()
        goes.start()
    for copy in stores:
        copy.wait()


def per_device(
    coupling,
    coupling_index,
    near_cost,
    near_index,
    source_weights,
    target_cost,
    target_index,
    target_weights,
):
    vmem = pl.BlockSpec(memory_space=pltpu.VMEM)
    anywhere = pl.BlockSpec(memory_space=pl.ANY)
    dma = pltpu.SemaphoreType.DMA
    moves = len(NUMBER)
    blocks = ROWS * SLOTS
    cost, source, target = pl.pallas_call(
        kernel,
        out_shape=(
            jax.ShapeDtypeStruct((blocks, BLK, BLK), f32),
            jax.ShapeDtypeStruct((ROWS, BLK), f32),
            jax.ShapeDtypeStruct((1, BLK), f32),
        ),
        in_specs=[anywhere] * 8,
        out_specs=(anywhere, vmem, vmem),
        scratch_shapes=[
            pltpu.SMEM((SLOTS, ROWS), jnp.int32),
            pltpu.SMEM((NEAR, ROWS), jnp.int32),
            pltpu.SMEM((LINKS, 1, GB), jnp.int32),
            pltpu.VMEM((ROWS, BLK), jnp.int32),
            pltpu.VMEM((1, BLK), jnp.int32),
            pltpu.VMEM((ROWS * NEAR, BLK, BLK), f32),
            pltpu.VMEM((blocks, BLK, BLK), f32),
            pltpu.VMEM((ROWS, BLK, 2 * BLK), bf16),
            pltpu.VMEM((ROWS, BLK, 2 * BLK), bf16),
            pltpu.VMEM((ROWS, 2 * BLK, 6 * BLK), bf16),
            pltpu.VMEM((ROWS, BLK, BLK), f32),
            pltpu.VMEM((GB * SHARD, BLK), f32),
            pltpu.VMEM((GB * LINKS + 1, BLK, BLK), bf16),
            pltpu.VMEM((GB * LINKS + 1, BLK, BLK), bf16),
            pltpu.VMEM((ROWS, BLK), f32),
            pltpu.VMEM((ROWS, 1, BLK), f32),
            pltpu.VMEM((1, BLK), f32),
            pltpu.VMEM((4, 1, BLK), f32),
            pltpu.VMEM((2, 4, 4, 8, BLK), f32),
            pltpu.VMEM((GB, 1, BLK), f32),
            pltpu.VMEM((ROWS, BLK), f32),
            pltpu.VMEM((GB, BLK), f32),
            pltpu.VMEM((ITERS, ROWS, BLK), f32),
            pltpu.VMEM((ITERS, 3, ROWS, BLK), f32),
            pltpu.VMEM((ROWS, BLK), f32),
            pltpu.VMEM((ITERS, GB, BLK), f32),
            pltpu.VMEM((ITERS, 16, BLK), f32),
            pltpu.VMEM((ITERS, 16, BLK), f32),
            pltpu.VMEM((ITERS, 15, 16, BLK), f32),
            pltpu.VMEM((ITERS + 1, GB, 1, BLK), f32),
            pltpu.VMEM((blocks, BLK), f32),
            pltpu.VMEM((blocks, BLK), f32),
            pltpu.VMEM((GB, 1, BLK), f32),
            dma((15,)),
            dma((moves,)),
            dma((moves,)),
            dma((moves + 1,)),
            dma((moves + 1,)),
            dma((4,)),
            dma((4,)),
            dma((7,)),
            dma((7,)),
            dma((ITERS, 2, 4)),
            dma((ITERS, 2, 4)),
            dma((ITERS,)),
            dma((ITERS,)),
            dma((ITERS, 16)),
            dma((ITERS, 16)),
            dma((ITERS,)),
            dma((ITERS,)),
        ],
        compiler_params=pltpu.CompilerParams(
            collective_id=0, has_side_effects=True, vmem_limit_bytes=60 * 2**20
        ),
        name="gromov_step",
    )(
        coupling_index.transpose(1, 2, 0).reshape(SLOTS, ROWS),
        near_index.T,
        target_index.transpose(2, 0, 1),
        source_weights.reshape(ROWS, BLK),
        target_weights,
        coupling.reshape(blocks, BLK, BLK),
        near_cost.reshape(ROWS * NEAR, BLK, BLK),
        target_cost.reshape(SHARD, BLK),
    )
    cost, source, target = pl.pallas_call(
        hand_over,
        out_shape=tuple(jax.ShapeDtypeStruct(x.shape, x.dtype) for x in (cost, source, target)),
        in_specs=[anywhere] * 3,
        out_specs=(anywhere,) * 3,
        scratch_shapes=[
            pltpu.VMEM((blocks, BLK, BLK), f32),
            pltpu.VMEM((ROWS, BLK), f32),
            pltpu.VMEM((1, BLK), f32),
            dma((6,)),
            dma((6,)),
        ],
        compiler_params=pltpu.CompilerParams(vmem_limit_bytes=60 * 2**20),
        name="hand_over",
    )(cost, source, target)
    return (
        cost.reshape(ROWS, 1, SLOTS, BLK, BLK),
        source.reshape(ROWS * BLK),
        target,
    )


def solution(mesh):
    placed = (
        P("rows", "cols", None, None, None),
        P("rows", "cols", None),
        P("rows", None, None, None),
        P("rows", None),
        P("rows"),
        P("cols", "rows", None, None, None),
        P("cols", None, None),
        P("cols", "rows"),
    )
    return jax.shard_map(
        per_device,
        mesh=mesh,
        in_specs=placed,
        out_specs=(P("rows", "cols", None, None, None), P("rows"), P("cols", "rows")),
        check_vma=False,
    )
```

```python
import functools
import itertools

import jax
import jax.numpy as jnp
from jax import lax
from jax.experimental import pallas as pl
from jax.experimental.pallas import tpu as pltpu
from jax.sharding import PartitionSpec as P

MESH = pl.DeviceIdType.MESH
BLK = 128
ROWS = 32
NEAR = 3
LINKS = 3
SLOTS = 2
GB = 32
ITERS = 3
SHARD = LINKS * BLK
HALF = SHARD // 2
QUARTER = SHARD // 4
COLS = 4
ENTROPY = 0.01
LOW = -1e30
f32 = jnp.float32
bf16 = jnp.bfloat16


def gather_plan():
    pieces = []
    for half, dz, dy, part in itertools.product(range(2), range(4), range(4), range(2)):
        if dz == 0 and dy == 0:
            continue
        first_axis = dy if half == 0 else dz
        last_axis = dz if half == 0 else dy
        axis = ("z" if half == 0 else "y") if last_axis else ("y" if half == 0 else "z")
        far = last_axis if last_axis else first_axis
        side = {1: 1, 3: -1, 2: 2 * part - 1}[far]
        came = ((dz - side) % 4, dy) if axis == "z" else (dz, (dy - side) % 4)
        pieces.append((half, dz, dy, part, axis, side, came))

    def onward(piece):
        half, dz, dy, part = piece[:4]
        after = [p for p in pieces if p[0] == half and p[3] == part and p[6] == (dz, dy)]
        return max([1 + onward(p) for p in after], default=0)

    hops = {p: onward(p) for p in pieces}
    have = {(half, 0, 0, part): 0 for half in range(2) for part in range(2)}
    left = list(pieces)
    sends = []
    arrivals = []
    slot = 0
    while left:
        sends.append([])
        for link in itertools.product("yz", (1, -1)):
            ready = [
                p
                for p in left
                if (p[4], p[5]) == link and have.get((p[0],) + p[6] + (p[3],), slot + 1) <= slot
            ]
            if ready:
                best = max(ready, key=lambda p: (hops[p], -have[(p[0],) + p[6] + (p[3],)], -left.index(p)))
                left.remove(best)
                sends[-1].append(best)
                have[best[:4]] = slot + 1 + DELAY
                arrivals.append(best)
        slot += 1
    arrivals.sort(key=lambda p: have[p[:4]])
    takes = [[p for p in arrivals if have[p[:4]] == when] for when in range(slot + 1 + DELAY)]
    number = {p: n for n, p in enumerate(arrivals)}
    return number, sends, takes


DELAY = 3
PARTS = 4
FARTHEST_FIRST = sorted(range(1, 16), key=lambda n: abs(n // 4 - 2) + abs(n % 4 - 2))
NUMBER, SENDS, TAKES = gather_plan()


def split(value):
    high = value.astype(bf16)
    return high, (value - high.astype(f32)).astype(bf16)


def dot(a, b):
    return jnp.dot(a, b, preferred_element_type=f32)


def kernel(
    slots_hbm,
    near_index_hbm,
    links_hbm,
    source_hbm,
    weight_hbm,
    coupling_hbm,
    near_hbm,
    target_hbm,
    cost_hbm,
    source_out,
    target_out,
    slots,
    near,
    links,
    source_ref,
    weight_ref,
    near_cost,
    plan,
    plan_high,
    plan_low,
    partial,
    row_sum,
    gathered,
    far_high,
    far_low,
    source_float,
    source_rows,
    weight_float,
    weight_land,
    extra,
    column,
    log_source,
    log_target,
    row_lse,
    row_land,
    source_pot,
    half_out,
    half_land,
    merged,
    merged_land,
    target_pot,
    peaks,
    sums,
    best_rows,
    load_sem,
    gather_send,
    gather_recv,
    pair_send,
    pair_recv,
    early_send,
    early_recv,
    extra_send,
    extra_recv,
    row_send,
    row_recv,
    half_send,
    half_recv,
    merge_send,
    merge_recv,
    pot_send,
    pot_recv,
):
    cost = plan
    scaled = near_cost

    rank = lax.axis_index("rows")
    group = lax.axis_index("cols")
    z = rank // 8
    y = (rank // 2) % 4
    core = rank % 2

    def at(dz, dy, other=0):
        return (((z + dz) % 4) * 4 + (y + dy) % 4) * 2 + (core + other) % 2

    def device(dz, dy, other=0, dx=0):
        return (at(dz, dy, other), (group + dx) % COLS)

    def remote(src, dst, send, recv, where):
        return pltpu.make_async_remote_copy(
            src_ref=src, dst_ref=dst, send_sem=send, recv_sem=recv, device_id=where, device_id_type=MESH
        )

    def piece_rows(dz, dy, half, part, other=0):
        first = at(dz, dy, other) * SHARD + half * HALF + part * QUARTER
        return gathered.at[pl.ds(pl.multiple_of(first, 8), QUARTER)]

    loads = []
    chunk = ROWS // 4
    for part in range(4):
        loads.append(
            pltpu.make_async_copy(
                coupling_hbm.at[pl.ds(part * chunk * SLOTS, chunk * SLOTS)],
                plan.at[pl.ds(part * chunk * SLOTS, chunk * SLOTS)],
                load_sem.at[part],
            )
        )
    for part in range(4):
        loads.append(
            pltpu.make_async_copy(
                near_hbm.at[pl.ds(part * chunk * NEAR, chunk * NEAR)],
                near_cost.at[pl.ds(part * chunk * NEAR, chunk * NEAR)],
                load_sem.at[4 + part],
            )
        )
    small = []
    for number, (src, dst) in enumerate(
        [
            (weight_hbm, weight_ref),
            (source_hbm, source_ref),
            (near_index_hbm, near),
            (slots_hbm, slots),
            (links_hbm, links),
        ]
    ):
        small.append(pltpu.make_async_copy(src, dst, load_sem.at[10 + number]))
    own_rows = gathered.at[pl.ds(pl.multiple_of(rank * SHARD, 8), SHARD)]
    own_load = pltpu.make_async_copy(target_hbm, own_rows, load_sem.at[8])

    barrier = pltpu.get_barrier_semaphore()
    neighbours = [device(0, 0, 1), device(0, 1), device(0, 3), device(1, 0), device(3, 0)]
    neighbours += [device(0, 0, 0, dx) for dx in (1, 3)]
    for where in neighbours:
        pl.semaphore_signal(barrier, inc=1, device_id=where, device_id_type=MESH)
    for copy in small + [own_load] + loads:
        copy.start()
    small[0].wait()
    weight_float[...] = weight_ref[...].astype(f32)
    pl.semaphore_wait(barrier, len(neighbours))

    started = []

    def start(copy):
        copy.start()
        started.append(copy)

    def send(piece):
        half, dz, dy, part, axis, side, came = piece
        dst = piece_rows(*came, half, part)
        if came == (0, 0):
            src = target_hbm.at[pl.ds(half * HALF + part * QUARTER, QUARTER)]
        else:
            src = dst
        number = NUMBER[piece]
        where = device(-side, 0) if axis == "z" else device(0, -side)
        start(remote(src, dst, gather_send.at[number], gather_recv.at[number], where))

    def split_rows(owner, half, part):
        first = half * HALF + part * QUARTER
        end = first + QUARTER
        while first < end:
            link = first // BLK
            size = min(end, (link + 1) * BLK) - first
            high, low = split(gathered[pl.ds(pl.multiple_of(owner * SHARD + first, 8), size), :])
            far_high[owner * LINKS + link, first - link * BLK : first - link * BLK + size, :] = high
            far_low[owner * LINKS + link, first - link * BLK : first - link * BLK + size, :] = low
            first += size

    def pair_copy(piece, other):
        here = piece_rows(piece[1], piece[2], piece[0], piece[3], other)
        number = NUMBER[piece]
        return remote(here, here, pair_send.at[number], pair_recv.at[number], device(0, 0, 1))

    def take(slot):
        pieces = TAKES[slot] if slot < len(TAKES) else []
        for piece in pieces:
            half, dz, dy, part = piece[:4]
            here = piece_rows(dz, dy, half, part)
            number = NUMBER[piece]
            remote(here, here, gather_send.at[number], gather_recv.at[number], device(0, 0, 1)).wait_recv()
            start(pair_copy(piece, 0))
        return pieces

    def use(pieces, other):
        for piece in pieces:
            if other:
                pair_copy(piece, 1).wait_recv()
            split_rows(at(piece[1], piece[2], other), piece[0], piece[3])

    def slot_at(row, slot):
        wanted = slots[slot, row]
        return lax.rem(wanted, 2) * 16 + lax.div(wanted, 2)

    def block_at(far, wanted):
        found = jnp.int32(GB * LINKS)
        for link in range(LINKS):
            found = jnp.where(links[link, 0, far] == wanted, far * LINKS + link, found)
        return found

    def split_plan(row, _):
        for q in range(SLOTS):
            high, low = split(plan[row * SLOTS + q])
            plan_high[row, :, q * BLK : (q + 1) * BLK] = high
            plan_low[row, :, q * BLK : (q + 1) * BLK] = low
        return 0

    def first_product(pair, _):
        for row in (2 * pair, 2 * pair + 1):
            total = jnp.zeros((BLK, BLK), f32)
            for k in range(NEAR):
                other = lax.rem(near[k, row], ROWS)
                block = near_cost[row * NEAR + k]
                high, low = split(block)
                high_plan = plan_high[other]
                low_plan = plan_low[other]
                both = jnp.concatenate([high, low], axis=1)
                result = dot(both, jnp.concatenate([high_plan, high_plan], axis=0)) + dot(high, low_plan)
                result_high, result_low = split(result)
                partial[row, 0:BLK, k * 2 * BLK : (k + 1) * 2 * BLK] = result_high
                partial[row, BLK : 2 * BLK, k * 2 * BLK : (k + 1) * 2 * BLK] = result_low
                total = total + block * block * source_rows[other]
            row_sum[row] = jnp.broadcast_to(jnp.sum(total, axis=1, keepdims=True), (BLK, BLK))
        return 0

    def first_rows(low, high):
        for part in range(4):
            if low <= part * chunk < high:
                loads[4 + part].wait()
        lax.fori_loop(low // 2, high // 2, first_product, 0)

    def plan_rows(part):
        loads[part].wait()
        lax.fori_loop(part * chunk, (part + 1) * chunk, split_plan, 0)

    def own_share():
        own_load.wait()
        own_weight = weight_float[...]
        weight_column = jnp.broadcast_to(own_weight, (BLK, BLK)).T
        extra_rows = [own_weight]
        for link in range(LINKS):
            block = gathered[pl.ds(pl.multiple_of(rank * SHARD + link * BLK, 8), BLK), :]
            extra_rows.append(jnp.sum(block * block * weight_column, axis=0, keepdims=True))
        across = own_weight
        for dx in (3, 2):
            early(dx).wait_recv()
        for dx in (1, 2, 3):
            across = across + weight_land[dx]
        extra_rows.append(across)
        extra_rows.append(jnp.sum(source_float[...], axis=0, keepdims=True))
        extra_rows.append(jnp.zeros((2, BLK), f32))
        extra[core, z, y] = jnp.concatenate(extra_rows, axis=0)

    def early(dx):
        src = weight_land.at[1] if dx == 2 else weight_float
        where = device(0, 0, 0, 1 if dx == 2 else dx)
        return remote(src, weight_land.at[dx], early_send.at[dx], early_recv.at[dx], where)

    def extra_copy(number):
        if number == 0:
            here, where = extra.at[core], device(0, 0, 1)
        elif number < 4:
            here, where = extra.at[core, z, y], device(0, number)
        else:
            here, where = extra.at[core, z], device(number - 3, 0)
        return remote(here, here, extra_send.at[number], extra_recv.at[number], where)

    position = lax.broadcasted_iota(jnp.int32, (GB, BLK), 0)
    row_scale_at = []

    def masses():
        everything = extra[...].reshape(GB, 8, BLK)
        target_total = jnp.sum(everything[:, 4, :])
        source_total = jnp.sum(everything[:, 5, :])
        target_scale = (COLS * GB * BLK) / target_total
        source_scale = (GB * ROWS * BLK) / source_total
        log_source[...] = jnp.log(source_float[...] * source_scale)
        log_target[...] = jnp.log(everything[:, 0, :] * target_scale)
        column_scale = target_scale / (LINKS * BLK)
        row_scale = source_scale / (NEAR * BLK)

        def add_column(step, total):
            own = (step % 16) * 2 + step // 16
            for link in range(LINKS):
                lands = links[link, 0, own]
                lands = lax.rem(lands, 2) * 16 + lax.div(lands, 2)
                value = extra[step // 16, (step // 4) % 4, step % 4, 1 + link : 2 + link, :]
                total = total + jnp.where(position == lands, value, 0.0)
            return total

        column_term = lax.fori_loop(0, GB, add_column, jnp.zeros((GB, BLK), f32), unroll=4) * column_scale
        column[...] = column_term.reshape(GB, 1, BLK)
        row_scale_at.append(row_scale)

    pair_own = len(NUMBER)
    from_pair = []
    rows_done = 0
    for slot in range(len(TAKES) + 2):
        taken = take(slot)
        if slot < len(SENDS):
            for piece in SENDS[slot]:
                send(piece)
        if slot == 0:
            plan_rows(0)
            plan_rows(1)
            for copy in small[1:]:
                copy.wait()
            source_float[...] = source_ref[...].astype(f32)
            source_rows[...] = source_float[...].reshape(ROWS, 1, BLK)
        elif slot == 1:
            plan_rows(2)
            plan_rows(3)
            own_rows = gathered.at[pl.ds(pl.multiple_of(rank * SHARD, 8), SHARD)]
            start(remote(target_hbm, own_rows, pair_send.at[pair_own], pair_recv.at[pair_own], device(0, 0, 1)))
            start(early(1))
            start(early(3))
        elif slot == 4:
            early(1).wait_recv()
            start(early(2))
        elif slot == 6:
            own_share()
            for half, part in itertools.product(range(2), range(2)):
                split_rows(rank, half, part)
        elif slot == 8:
            for number in (1, 2, 3):
                start(extra_copy(number))
        elif slot == 11:
            for number in (1, 2, 3):
                extra_copy(number).wait_recv()
            for number in (4, 5, 6):
                start(extra_copy(number))
        elif slot == 15:
            for number in (4, 5, 6):
                extra_copy(number).wait_recv()
            start(extra_copy(0))
        use(taken, 0)
        from_pair.append(taken)
        if slot >= 2:
            use(from_pair[slot - 2], 1)
        if slot >= 2 and rows_done < ROWS:
            more = min(ROWS, rows_done + 4)
            first_rows(rows_done, more)
            rows_done = more
    here = gathered.at[pl.ds(pl.multiple_of(at(0, 0, 1) * SHARD, 8), SHARD)]
    remote(here, here, pair_send.at[pair_own], pair_recv.at[pair_own], device(0, 0, 1)).wait_recv()
    for half, part in itertools.product(range(2), range(2)):
        split_rows(at(0, 0, 1), half, part)
    extra_copy(0).wait_recv()
    masses()
    far_high[GB * LINKS] = jnp.zeros((BLK, BLK), bf16)
    far_low[GB * LINKS] = jnp.zeros((BLK, BLK), bf16)

    factor = 2.0 / (NEAR * BLK) / (COLS * SLOTS * BLK)

    def second_row(row):
        high_rows = []
        low_rows = []
        wanted = [slots[slot, row] for slot in range(SLOTS)]
        for k in range(NEAR):
            other = lax.rem(near[k, row], ROWS)
            for q in range(SLOTS):
                far = slots[q, other]
                found = [block_at(far, wanted[slot]) for slot in range(SLOTS)]
                high_rows.append(jnp.concatenate([far_high[n] for n in found], axis=1))
                low_rows.append(jnp.concatenate([far_low[n] for n in found], axis=1))
        result = dot(partial[row], jnp.concatenate(high_rows, axis=0))
        result = result[0:BLK] + result[BLK : 2 * BLK]
        result = result + dot(partial[row, 0:BLK, :], jnp.concatenate(low_rows, axis=0))
        across = row_sum[row] * row_scale_at[0]
        scores = []
        for slot in range(SLOTS):
            own_column = column[slot_at(row, slot)]
            value = across + own_column - factor * result[:, slot * BLK : (slot + 1) * BLK]
            cost[row * SLOTS + slot] = value
            value = value * (1.0 / ENTROPY)
            scaled[row * SLOTS + slot] = value
            scores.append(-value)
        return scores

    def row_sums(scores):
        top = jnp.max(jnp.maximum(scores[0], scores[1]), axis=1, keepdims=True)
        total = jnp.sum(jnp.exp(scores[0] - top) + jnp.exp(scores[1] - top), axis=1, keepdims=True)
        return top, total

    def row_result(found):
        tops = jnp.concatenate([top for top, _ in found], axis=1).T
        totals = jnp.concatenate([total for _, total in found], axis=1).T
        return tops + jnp.log(totals)

    part_rows = ROWS // PARTS

    def row_copy(step, part, dx):
        rows = pl.ds(pl.multiple_of(part * part_rows, part_rows), part_rows)
        return remote(
            row_lse.at[step, rows],
            row_land.at[step, dx - 1, rows],
            row_send.at[step, part, dx],
            row_recv.at[step, part, dx],
            device(0, 0, 0, dx),
        )

    def send_rows(step, part, found):
        row_lse[step, pl.ds(pl.multiple_of(part * part_rows, part_rows), part_rows), :] = row_result(found)
        for dx in (2, 1, 3):
            row_copy(step, part, dx).start()

    def second_product(part, _):
        send_rows(0, part, [row_sums(second_row(part * part_rows + inner)) for inner in range(part_rows)])
        return 0

    lax.fori_loop(0, PARTS, second_product, 0)
    out_copy = pltpu.make_async_copy(cost, cost_hbm, load_sem.at[9])
    out_copy.start()

    mine = core * 16
    theirs = 16 - mine
    def row_pass(step, part):
        found = []
        for row in range(part * part_rows, (part + 1) * part_rows):
            found.append(
                row_sums(
                    [
                        target_pot[step, slot_at(row, slot)] - scaled[row * SLOTS + slot]
                        for slot in range(SLOTS)
                    ]
                )
            )
        send_rows(step, part, found)

    def column_pass(part, best):
        potentials = source_pot[part * part_rows : (part + 1) * part_rows, :].T
        for inner in range(part_rows):
            row = part * part_rows + inner
            potential = potentials[:, inner : inner + 1]
            for slot in range(SLOTS):
                block = row * SLOTS + slot
                scores = potential - scaled[block]
                top = jnp.max(scores, axis=0, keepdims=True)
                total = jnp.sum(jnp.exp(scores - top), axis=0, keepdims=True)
                peaks[block : block + 1, :] = top
                sums[block : block + 1, :] = total
                best = jnp.where(position == slot_at(row, slot), jnp.maximum(best, top), best)
        return best

    def column_result(best):
        best_rows[...] = best.reshape(GB, 1, BLK)
        every = [(row, slot) for row in range(ROWS) for slot in range(SLOTS)]
        tops = jnp.concatenate([best_rows[slot_at(row, slot)] for row, slot in every], axis=0)
        values = sums[...] * jnp.exp(peaks[...] - tops)
        total = jnp.zeros((GB, BLK), f32)
        for block, (row, slot) in enumerate(every):
            total = total + jnp.where(position == slot_at(row, slot), values[block : block + 1, :], 0.0)
        return jnp.where(total > 0.0, best + jnp.log(jnp.maximum(total, 1e-30)), LOW)

    def merge(values):
        top = functools.reduce(jnp.maximum, values)
        total = functools.reduce(jnp.add, [jnp.exp(value - top) for value in values])
        return top + jnp.log(total)

    def iteration(step, _):
        moved = []

        def move(copy):
            copy.start()
            moved.append(copy)
            return copy

        for part in range(PARTS):
            pl.when(step > 0)(functools.partial(row_pass, step, part))
        best = jnp.full((GB, BLK), LOW, f32)
        for part in range(PARTS):
            for dx in (1, 3, 2):
                row_copy(step, part, dx).wait_recv()
            rows = slice(part * part_rows, (part + 1) * part_rows)
            arrived = [row_lse[step, rows, :]] + [row_land[step, n, rows, :] for n in range(3)]
            source_pot[rows, :] = log_source[rows, :] - merge(arrived)
            best = column_pass(part, best)
        half_out[step] = column_result(best)
        move(
            remote(
                half_out.at[step, pl.ds(pl.multiple_of(theirs, 16), 16)],
                half_land.at[step],
                half_send.at[step],
                half_recv.at[step],
                device(0, 0, 1),
            )
        ).wait_recv()
        own = half_out[step, pl.ds(pl.multiple_of(mine, 16), 16), :]
        merged[step] = merge([own, half_land[step]])
        row_sent = [row_copy(step, part, dx) for part in range(PARTS) for dx in (1, 2, 3)]

        def exchange(pieces):
            copies = []
            for number in FARTHEST_FIRST:
                src, dst = pieces(number)
                copies.append(
                    remote(
                        src,
                        dst,
                        merge_send.at[step, number],
                        merge_recv.at[step, number],
                        device(number // 4, number % 4),
                    )
                )
                copies[-1].start()
            for copy in copies:
                copy.wait_recv()
            for copy in copies:
                copy.wait_send()

        @pl.when(step < ITERS - 1)
        def _():
            exchange(lambda number: (merged.at[step], merged_land.at[step, number - 1]))
            total = merge([merged[step]] + [merged_land[step, n] for n in range(15)])
            own = log_target[pl.ds(pl.multiple_of(mine, 16), 16), :] - total
            here = target_pot.at[step + 1, pl.ds(pl.multiple_of(mine, 16), 16)]
            here[...] = own.reshape(16, 1, BLK)
            copy = remote(here, here, pot_send.at[step], pot_recv.at[step], device(0, 0, 1))
            copy.start()
            copy.wait_recv()
            copy.wait_send()

        @pl.when(step == ITERS - 1)
        def _():
            def pieces(number):
                theirs_at = ((z + number // 4) % 4) * 4 + (y + number % 4) % 4
                return merged.at[step, pl.ds(theirs_at, 1)], merged_land.at[step, number - 1, pl.ds(0, 1)]

            exchange(pieces)
            own = z * 4 + y
            arrived = [merged_land[step, n, 0:1, :] for n in range(15)]
            total = merge([merged[step, pl.ds(own, 1), :]] + arrived)
            target_out[...] = (log_target[pl.ds(mine + own, 1), :] - total) * ENTROPY

        for copy in row_sent:
            copy.wait_send()
        for copy in moved:
            copy.wait_send()
        return 0

    lax.fori_loop(0, ITERS, iteration, 0)
    source_out[...] = source_pot[...] * ENTROPY
    for copy in started:
        copy.wait_send()
    out_copy.wait()


def hand_over(cost, source, target, cost_out, source_out, target_out, held, source_held, target_held, load, store):
    parts = 4
    size = held.shape[0] // parts
    rows = [pl.ds(n * size, size) for n in range(parts)]
    steps = [(cost.at[r], held.at[r], cost_out.at[r]) for r in rows]
    steps[1:1] = [(source, source_held, source_out), (target, target_held, target_out)]
    loads = [pltpu.make_async_copy(src, here, load.at[n]) for n, (src, here, _) in enumerate(steps)]
    stores = [pltpu.make_async_copy(here, dst, store.at[n]) for n, (_, here, dst) in enumerate(steps)]
    for copy in loads:
        copy.start()
    for came, goes in zip(loads, stores):
        came.wait()
        goes.start()
    for copy in stores:
        copy.wait()


def per_device(
    coupling,
    coupling_index,
    near_cost,
    near_index,
    source_weights,
    target_cost,
    target_index,
    target_weights,
):
    vmem = pl.BlockSpec(memory_space=pltpu.VMEM)
    anywhere = pl.BlockSpec(memory_space=pl.ANY)
    dma = pltpu.SemaphoreType.DMA
    moves = len(NUMBER)
    blocks = ROWS * SLOTS
    cost, source, target = pl.pallas_call(
        kernel,
        out_shape=(
            jax.ShapeDtypeStruct((blocks, BLK, BLK), f32),
            jax.ShapeDtypeStruct((ROWS, BLK), f32),
            jax.ShapeDtypeStruct((1, BLK), f32),
        ),
        in_specs=[anywhere] * 8,
        out_specs=(anywhere, vmem, vmem),
        scratch_shapes=[
            pltpu.SMEM((SLOTS, ROWS), jnp.int32),
            pltpu.SMEM((NEAR, ROWS), jnp.int32),
            pltpu.SMEM((LINKS, 1, GB), jnp.int32),
            pltpu.VMEM((ROWS, BLK), jnp.int32),
            pltpu.VMEM((1, BLK), jnp.int32),
            pltpu.VMEM((ROWS * NEAR, BLK, BLK), f32),
            pltpu.VMEM((blocks, BLK, BLK), f32),
            pltpu.VMEM((ROWS, BLK, 2 * BLK), bf16),
            pltpu.VMEM((ROWS, BLK, 2 * BLK), bf16),
            pltpu.VMEM((ROWS, 2 * BLK, 6 * BLK), bf16),
            pltpu.VMEM((ROWS, BLK, BLK), f32),
            pltpu.VMEM((GB * SHARD, BLK), f32),
            pltpu.VMEM((GB * LINKS + 1, BLK, BLK), bf16),
            pltpu.VMEM((GB * LINKS + 1, BLK, BLK), bf16),
            pltpu.VMEM((ROWS, BLK), f32),
            pltpu.VMEM((ROWS, 1, BLK), f32),
            pltpu.VMEM((1, BLK), f32),
            pltpu.VMEM((4, 1, BLK), f32),
            pltpu.VMEM((2, 4, 4, 8, BLK), f32),
            pltpu.VMEM((GB, 1, BLK), f32),
            pltpu.VMEM((ROWS, BLK), f32),
            pltpu.VMEM((GB, BLK), f32),
            pltpu.VMEM((ITERS, ROWS, BLK), f32),
            pltpu.VMEM((ITERS, 3, ROWS, BLK), f32),
            pltpu.VMEM((ROWS, BLK), f32),
            pltpu.VMEM((ITERS, GB, BLK), f32),
            pltpu.VMEM((ITERS, 16, BLK), f32),
            pltpu.VMEM((ITERS, 16, BLK), f32),
            pltpu.VMEM((ITERS, 15, 16, BLK), f32),
            pltpu.VMEM((ITERS + 1, GB, 1, BLK), f32),
            pltpu.VMEM((blocks, BLK), f32),
            pltpu.VMEM((blocks, BLK), f32),
            pltpu.VMEM((GB, 1, BLK), f32),
            dma((15,)),
            dma((moves,)),
            dma((moves,)),
            dma((moves + 1,)),
            dma((moves + 1,)),
            dma((4,)),
            dma((4,)),
            dma((7,)),
            dma((7,)),
            dma((ITERS, PARTS, 4)),
            dma((ITERS, PARTS, 4)),
            dma((ITERS,)),
            dma((ITERS,)),
            dma((ITERS, 16)),
            dma((ITERS, 16)),
            dma((ITERS,)),
            dma((ITERS,)),
        ],
        compiler_params=pltpu.CompilerParams(
            collective_id=0, has_side_effects=True, vmem_limit_bytes=60 * 2**20
        ),
        name="gromov_step",
    )(
        coupling_index.transpose(1, 2, 0).reshape(SLOTS, ROWS),
        near_index.T,
        target_index.transpose(2, 0, 1),
        source_weights.reshape(ROWS, BLK),
        target_weights,
        coupling.reshape(blocks, BLK, BLK),
        near_cost.reshape(ROWS * NEAR, BLK, BLK),
        target_cost.reshape(SHARD, BLK),
    )
    cost, source, target = pl.pallas_call(
        hand_over,
        out_shape=tuple(jax.ShapeDtypeStruct(x.shape, x.dtype) for x in (cost, source, target)),
        in_specs=[anywhere] * 3,
        out_specs=(anywhere,) * 3,
        scratch_shapes=[
            pltpu.VMEM((blocks, BLK, BLK), f32),
            pltpu.VMEM((ROWS, BLK), f32),
            pltpu.VMEM((1, BLK), f32),
            dma((6,)),
            dma((6,)),
        ],
        compiler_params=pltpu.CompilerParams(vmem_limit_bytes=60 * 2**20),
        name="hand_over",
    )(cost, source, target)
    return (
        cost.reshape(ROWS, 1, SLOTS, BLK, BLK),
        source.reshape(ROWS * BLK),
        target,
    )


def solution(mesh):
    placed = (
        P("rows", "cols", None, None, None),
        P("rows", "cols", None),
        P("rows", None, None, None),
        P("rows", None),
        P("rows"),
        P("cols", "rows", None, None, None),
        P("cols", None, None),
        P("cols", "rows"),
    )
    return jax.shard_map(
        per_device,
        mesh=mesh,
        in_specs=placed,
        out_specs=(P("rows", "cols", None, None, None), P("rows"), P("cols", "rows")),
        check_vma=False,
    )
```

```python
import functools
import itertools

import jax
import jax.numpy as jnp
from jax import lax
from jax.experimental import pallas as pl
from jax.experimental.pallas import tpu as pltpu
from jax.sharding import PartitionSpec as P

MESH = pl.DeviceIdType.MESH
BLK = 128
ROWS = 32
NEAR = 3
LINKS = 3
SLOTS = 2
GB = 32
ITERS = 3
SHARD = LINKS * BLK
HALF = SHARD // 2
QUARTER = SHARD // 4
COLS = 4
ENTROPY = 0.01
LOW = -1e30
f32 = jnp.float32
bf16 = jnp.bfloat16


def gather_plan():
    pieces = []
    for half, dz, dy, part in itertools.product(range(2), range(4), range(4), range(2)):
        if dz == 0 and dy == 0:
            continue
        first_axis = dy if half == 0 else dz
        last_axis = dz if half == 0 else dy
        axis = ("z" if half == 0 else "y") if last_axis else ("y" if half == 0 else "z")
        far = last_axis if last_axis else first_axis
        side = {1: 1, 3: -1, 2: 2 * part - 1}[far]
        came = ((dz - side) % 4, dy) if axis == "z" else (dz, (dy - side) % 4)
        pieces.append((half, dz, dy, part, axis, side, came))

    def onward(piece):
        half, dz, dy, part = piece[:4]
        after = [p for p in pieces if p[0] == half and p[3] == part and p[6] == (dz, dy)]
        return max([1 + onward(p) for p in after], default=0)

    hops = {p: onward(p) for p in pieces}
    have = {(half, 0, 0, part): 0 for half in range(2) for part in range(2)}
    left = list(pieces)
    sends = []
    arrivals = []
    slot = 0
    while left:
        sends.append([])
        for link in itertools.product("yz", (1, -1)):
            ready = [
                p
                for p in left
                if (p[4], p[5]) == link and have.get((p[0],) + p[6] + (p[3],), slot + 1) <= slot
            ]
            if ready:
                best = max(ready, key=lambda p: (hops[p], -have[(p[0],) + p[6] + (p[3],)], -left.index(p)))
                left.remove(best)
                sends[-1].append(best)
                have[best[:4]] = slot + 1 + DELAY
                arrivals.append(best)
        slot += 1
    arrivals.sort(key=lambda p: have[p[:4]])
    takes = [[p for p in arrivals if have[p[:4]] == when] for when in range(slot + 1 + DELAY)]
    number = {p: n for n, p in enumerate(arrivals)}
    return number, sends, takes


DELAY = 3
PARTS = 4
FARTHEST_FIRST = sorted(range(1, 16), key=lambda n: abs(n // 4 - 2) + abs(n % 4 - 2))
NUMBER, SENDS, TAKES = gather_plan()


def split(value):
    high = value.astype(bf16)
    return high, (value - high.astype(f32)).astype(bf16)


def dot(a, b):
    return jnp.dot(a, b, preferred_element_type=f32)


def kernel(
    slots_hbm,
    near_index_hbm,
    links_hbm,
    source_hbm,
    weight_hbm,
    coupling_hbm,
    near_hbm,
    target_hbm,
    cost_hbm,
    source_out,
    target_out,
    slots,
    near,
    links,
    source_ref,
    weight_ref,
    near_cost,
    plan,
    plan_high,
    plan_low,
    partial,
    row_sum,
    gathered,
    far_high,
    far_low,
    shifted,
    source_float,
    source_rows,
    weight_float,
    weight_land,
    extra,
    column,
    log_source,
    log_target,
    row_lse,
    row_land,
    source_pot,
    half_out,
    half_land,
    merged,
    merged_land,
    target_pot,
    peaks,
    sums,
    best_rows,
    load_sem,
    gather_send,
    gather_recv,
    pair_send,
    pair_recv,
    early_send,
    early_recv,
    extra_send,
    extra_recv,
    row_send,
    row_recv,
    half_send,
    half_recv,
    merge_send,
    merge_recv,
    pot_send,
    pot_recv,
):
    cost = plan
    scaled = near_cost

    rank = lax.axis_index("rows")
    group = lax.axis_index("cols")
    z = rank // 8
    y = (rank // 2) % 4
    core = rank % 2

    def at(dz, dy, other=0):
        return (((z + dz) % 4) * 4 + (y + dy) % 4) * 2 + (core + other) % 2

    def device(dz, dy, other=0, dx=0):
        return (at(dz, dy, other), (group + dx) % COLS)

    def remote(src, dst, send, recv, where):
        return pltpu.make_async_remote_copy(
            src_ref=src, dst_ref=dst, send_sem=send, recv_sem=recv, device_id=where, device_id_type=MESH
        )

    def piece_rows(dz, dy, half, part, other=0):
        first = at(dz, dy, other) * SHARD + half * HALF + part * QUARTER
        return gathered.at[pl.ds(pl.multiple_of(first, 8), QUARTER)]

    loads = []
    chunk = ROWS // 4
    for part in range(4):
        loads.append(
            pltpu.make_async_copy(
                coupling_hbm.at[pl.ds(part * chunk * SLOTS, chunk * SLOTS)],
                plan.at[pl.ds(part * chunk * SLOTS, chunk * SLOTS)],
                load_sem.at[part],
            )
        )
    for part in range(4):
        loads.append(
            pltpu.make_async_copy(
                near_hbm.at[pl.ds(part * chunk * NEAR, chunk * NEAR)],
                near_cost.at[pl.ds(part * chunk * NEAR, chunk * NEAR)],
                load_sem.at[4 + part],
            )
        )
    small = []
    for number, (src, dst) in enumerate(
        [
            (weight_hbm, weight_ref),
            (source_hbm, source_ref),
            (near_index_hbm, near),
            (slots_hbm, slots),
            (links_hbm, links),
        ]
    ):
        small.append(pltpu.make_async_copy(src, dst, load_sem.at[10 + number]))
    own_rows = gathered.at[pl.ds(pl.multiple_of(rank * SHARD, 8), SHARD)]
    own_load = pltpu.make_async_copy(target_hbm, own_rows, load_sem.at[8])

    barrier = pltpu.get_barrier_semaphore()
    neighbours = [device(0, 0, 1), device(0, 1), device(0, 3), device(1, 0), device(3, 0)]
    neighbours += [device(0, 0, 0, dx) for dx in (1, 3)]
    for where in neighbours:
        pl.semaphore_signal(barrier, inc=1, device_id=where, device_id_type=MESH)
    for copy in small + [own_load] + loads:
        copy.start()
    small[0].wait()
    weight_float[...] = weight_ref[...].astype(f32)
    pl.semaphore_wait(barrier, len(neighbours))

    started = []

    def start(copy):
        copy.start()
        started.append(copy)

    def send(piece):
        half, dz, dy, part, axis, side, came = piece
        dst = piece_rows(*came, half, part)
        if came == (0, 0):
            src = target_hbm.at[pl.ds(half * HALF + part * QUARTER, QUARTER)]
        else:
            src = dst
        number = NUMBER[piece]
        where = device(-side, 0) if axis == "z" else device(0, -side)
        start(remote(src, dst, gather_send.at[number], gather_recv.at[number], where))

    def split_rows(owner, half, part):
        first = half * HALF + part * QUARTER
        end = first + QUARTER
        while first < end:
            link = first // BLK
            size = min(end, (link + 1) * BLK) - first
            high, low = split(gathered[pl.ds(pl.multiple_of(owner * SHARD + first, 8), size), :])
            far_high[owner * LINKS + link, first - link * BLK : first - link * BLK + size, :] = high
            far_low[owner * LINKS + link, first - link * BLK : first - link * BLK + size, :] = low
            first += size

    def pair_copy(piece, other):
        here = piece_rows(piece[1], piece[2], piece[0], piece[3], other)
        number = NUMBER[piece]
        return remote(here, here, pair_send.at[number], pair_recv.at[number], device(0, 0, 1))

    def take(slot):
        pieces = TAKES[slot] if slot < len(TAKES) else []
        for piece in pieces:
            half, dz, dy, part = piece[:4]
            here = piece_rows(dz, dy, half, part)
            number = NUMBER[piece]
            remote(here, here, gather_send.at[number], gather_recv.at[number], device(0, 0, 1)).wait_recv()
            start(pair_copy(piece, 0))
        return pieces

    def use(pieces, other):
        for piece in pieces:
            if other:
                pair_copy(piece, 1).wait_recv()
            split_rows(at(piece[1], piece[2], other), piece[0], piece[3])

    def slot_at(row, slot):
        wanted = slots[slot, row]
        return lax.rem(wanted, 2) * 16 + lax.div(wanted, 2)

    def block_at(far, wanted):
        found = jnp.int32(GB * LINKS)
        for link in range(LINKS):
            found = jnp.where(links[link, 0, far] == wanted, far * LINKS + link, found)
        return found

    def split_plan(row, _):
        for q in range(SLOTS):
            high, low = split(plan[row * SLOTS + q])
            plan_high[row, :, q * BLK : (q + 1) * BLK] = high
            plan_low[row, :, q * BLK : (q + 1) * BLK] = low
        return 0

    def first_product(pair, _):
        for row in (2 * pair, 2 * pair + 1):
            total = jnp.zeros((BLK, BLK), f32)
            for k in range(NEAR):
                other = lax.rem(near[k, row], ROWS)
                block = near_cost[row * NEAR + k]
                high, low = split(block)
                high_plan = plan_high[other]
                low_plan = plan_low[other]
                both = jnp.concatenate([high, low], axis=1)
                result = dot(both, jnp.concatenate([high_plan, high_plan], axis=0)) + dot(high, low_plan)
                result_high, result_low = split(result)
                partial[row, 0:BLK, k * 2 * BLK : (k + 1) * 2 * BLK] = result_high
                partial[row, BLK : 2 * BLK, k * 2 * BLK : (k + 1) * 2 * BLK] = result_low
                total = total + block * block * source_rows[other]
            row_sum[row] = jnp.broadcast_to(jnp.sum(total, axis=1, keepdims=True), (BLK, BLK))
        return 0

    def first_rows(low, high):
        for part in range(4):
            if low <= part * chunk < high:
                loads[4 + part].wait()
        lax.fori_loop(low // 2, high // 2, first_product, 0)

    def plan_rows(part):
        loads[part].wait()
        lax.fori_loop(part * chunk, (part + 1) * chunk, split_plan, 0)

    def own_share():
        own_load.wait()
        own_weight = weight_float[...]
        weight_column = jnp.broadcast_to(own_weight, (BLK, BLK)).T
        extra_rows = [own_weight]
        for link in range(LINKS):
            block = gathered[pl.ds(pl.multiple_of(rank * SHARD + link * BLK, 8), BLK), :]
            extra_rows.append(jnp.sum(block * block * weight_column, axis=0, keepdims=True))
        across = own_weight
        for dx in (3, 2):
            early(dx).wait_recv()
        for dx in (1, 2, 3):
            across = across + weight_land[dx]
        extra_rows.append(across)
        extra_rows.append(jnp.sum(source_float[...], axis=0, keepdims=True))
        extra_rows.append(jnp.zeros((2, BLK), f32))
        extra[core, z, y] = jnp.concatenate(extra_rows, axis=0)

    def early(dx):
        src = weight_land.at[1] if dx == 2 else weight_float
        where = device(0, 0, 0, 1 if dx == 2 else dx)
        return remote(src, weight_land.at[dx], early_send.at[dx], early_recv.at[dx], where)

    def extra_copy(number):
        if number == 0:
            here, where = extra.at[core], device(0, 0, 1)
        elif number < 4:
            here, where = extra.at[core, z, y], device(0, number)
        else:
            here, where = extra.at[core, z], device(number - 3, 0)
        return remote(here, here, extra_send.at[number], extra_recv.at[number], where)

    position = lax.broadcasted_iota(jnp.int32, (GB, BLK), 0)
    row_scale_at = []

    def masses():
        everything = extra[...].reshape(GB, 8, BLK)
        target_total = jnp.sum(everything[:, 4, :])
        source_total = jnp.sum(everything[:, 5, :])
        target_scale = (COLS * GB * BLK) / target_total
        source_scale = (GB * ROWS * BLK) / source_total
        log_source[...] = jnp.log(source_float[...] * source_scale)
        log_target[...] = jnp.log(everything[:, 0, :] * target_scale)
        column_scale = target_scale / (LINKS * BLK)
        row_scale = source_scale / (NEAR * BLK)

        def add_column(step, total):
            own = (step % 16) * 2 + step // 16
            for link in range(LINKS):
                lands = links[link, 0, own]
                lands = lax.rem(lands, 2) * 16 + lax.div(lands, 2)
                value = extra[step // 16, (step // 4) % 4, step % 4, 1 + link : 2 + link, :]
                total = total + jnp.where(position == lands, value, 0.0)
            return total

        column_term = lax.fori_loop(0, GB, add_column, jnp.zeros((GB, BLK), f32), unroll=4) * column_scale
        column[...] = column_term.reshape(GB, 1, BLK)
        row_scale_at.append(row_scale)

    pair_own = len(NUMBER)
    from_pair = []
    rows_done = 0
    for slot in range(len(TAKES) + 2):
        taken = take(slot)
        if slot < len(SENDS):
            for piece in SENDS[slot]:
                send(piece)
        if slot == 0:
            plan_rows(0)
            plan_rows(1)
            for copy in small[1:]:
                copy.wait()
            source_float[...] = source_ref[...].astype(f32)
            source_rows[...] = source_float[...].reshape(ROWS, 1, BLK)
        elif slot == 1:
            plan_rows(2)
            plan_rows(3)
            own_rows = gathered.at[pl.ds(pl.multiple_of(rank * SHARD, 8), SHARD)]
            start(remote(target_hbm, own_rows, pair_send.at[pair_own], pair_recv.at[pair_own], device(0, 0, 1)))
            start(early(1))
            start(early(3))
        elif slot == 4:
            early(1).wait_recv()
            start(early(2))
        elif slot == 6:
            own_share()
            for half, part in itertools.product(range(2), range(2)):
                split_rows(rank, half, part)
        elif slot == 8:
            for number in (1, 2, 3):
                start(extra_copy(number))
        elif slot == 11:
            for number in (1, 2, 3):
                extra_copy(number).wait_recv()
            for number in (4, 5, 6):
                start(extra_copy(number))
        elif slot == 15:
            for number in (4, 5, 6):
                extra_copy(number).wait_recv()
            start(extra_copy(0))
        use(taken, 0)
        from_pair.append(taken)
        if slot >= 2:
            use(from_pair[slot - 2], 1)
        if slot >= 2 and rows_done < ROWS:
            more = min(ROWS, rows_done + 4)
            first_rows(rows_done, more)
            rows_done = more
    here = gathered.at[pl.ds(pl.multiple_of(at(0, 0, 1) * SHARD, 8), SHARD)]
    remote(here, here, pair_send.at[pair_own], pair_recv.at[pair_own], device(0, 0, 1)).wait_recv()
    for half, part in itertools.product(range(2), range(2)):
        split_rows(at(0, 0, 1), half, part)
    extra_copy(0).wait_recv()
    masses()
    far_high[GB * LINKS] = jnp.zeros((BLK, BLK), bf16)
    far_low[GB * LINKS] = jnp.zeros((BLK, BLK), bf16)

    factor = 2.0 / (NEAR * BLK) / (COLS * SLOTS * BLK)

    def second_row(row):
        high_rows = []
        low_rows = []
        wanted = [slots[slot, row] for slot in range(SLOTS)]
        for k in range(NEAR):
            other = lax.rem(near[k, row], ROWS)
            for q in range(SLOTS):
                far = slots[q, other]
                found = [block_at(far, wanted[slot]) for slot in range(SLOTS)]
                high_rows.append(jnp.concatenate([far_high[n] for n in found], axis=1))
                low_rows.append(jnp.concatenate([far_low[n] for n in found], axis=1))
        result = dot(partial[row], jnp.concatenate(high_rows, axis=0))
        result = result[0:BLK] + result[BLK : 2 * BLK]
        result = result + dot(partial[row, 0:BLK, :], jnp.concatenate(low_rows, axis=0))
        across = row_sum[row] * row_scale_at[0]
        scores = []
        for slot in range(SLOTS):
            own_column = column[slot_at(row, slot)]
            value = across + own_column - factor * result[:, slot * BLK : (slot + 1) * BLK]
            cost[row * SLOTS + slot] = value
            value = value * (1.0 / ENTROPY)
            scaled[row * SLOTS + slot] = value
            scores.append(-value)
        return scores

    def row_sums(scores):
        top = jnp.max(jnp.maximum(scores[0], scores[1]), axis=1, keepdims=True)
        total = jnp.sum(jnp.exp(scores[0] - top) + jnp.exp(scores[1] - top), axis=1, keepdims=True)
        return top, total

    def row_result(found):
        tops = jnp.concatenate([top for top, _ in found], axis=1).T
        totals = jnp.concatenate([total for _, total in found], axis=1).T
        return tops + jnp.log(totals)

    part_rows = ROWS // PARTS

    def row_copy(step, part, dx):
        rows = pl.ds(pl.multiple_of(part * part_rows, part_rows), part_rows)
        return remote(
            row_lse.at[step, rows],
            row_land.at[step, dx - 1, rows],
            row_send.at[step, part, dx],
            row_recv.at[step, part, dx],
            device(0, 0, 0, dx),
        )

    def send_rows(step, part, value):
        row_lse[step, pl.ds(pl.multiple_of(part * part_rows, part_rows), part_rows), :] = value
        for dx in (2, 1, 3):
            row_copy(step, part, dx).start()

    def second_product(part, _):
        found = [row_sums(second_row(part * part_rows + inner)) for inner in range(part_rows)]
        send_rows(0, part, row_result(found))
        return 0

    lax.fori_loop(0, PARTS, second_product, 0)
    out_copy = pltpu.make_async_copy(cost, cost_hbm, load_sem.at[9])
    out_copy.start()

    mine = core * 16
    theirs = 16 - mine
    half = pl.ds(pl.multiple_of(mine, 16), 16)
    other_half = pl.ds(pl.multiple_of(theirs, 16), 16)

    def row_pass(step, part):
        totals = []
        for inner in range(part_rows):
            row = part * part_rows + inner
            values = [
                jnp.exp(shifted[row * SLOTS + slot] + target_pot[step, slot_at(row, slot)]) for slot in range(SLOTS)
            ]
            totals.append(jnp.sum(values[0] + values[1], axis=1, keepdims=True))
        send_rows(step, part, jnp.concatenate(totals, axis=1).T)

    def merge(values):
        top = functools.reduce(jnp.maximum, values)
        total = functools.reduce(jnp.add, [jnp.exp(value - top) for value in values])
        return top + jnp.log(total)

    def add_up(values):
        return functools.reduce(jnp.add, values)

    def column_part(step, part, found):
        for dx in (1, 3, 2):
            row_copy(step, part, dx).wait_recv()
        rows = pl.ds(pl.multiple_of(part * part_rows, part_rows), part_rows)
        arrived = [row_lse[step, rows, :]] + [row_land[step, n, rows, :] for n in range(3)]
        if step == 0:
            potentials = log_source[rows, :] - merge(arrived)
        else:
            potentials = source_pot[rows, :] + (log_source[rows, :] - jnp.log(add_up(arrived)))
        source_pot[rows, :] = potentials
        potentials = potentials.T
        for inner in range(part_rows):
            row = part * part_rows + inner
            potential = potentials[:, inner : inner + 1]
            for slot in range(SLOTS):
                block = row * SLOTS + slot
                here = position == slot_at(row, slot)
                scores = potential - scaled[block]
                if step < ITERS - 1:
                    shifted[block] = scores
                if step == 0:
                    top = jnp.max(scores, axis=0, keepdims=True)
                    total = jnp.sum(jnp.exp(scores - top), axis=0, keepdims=True)
                    peaks[pl.ds(block, 1), :] = top
                    sums[pl.ds(block, 1), :] = total
                    found = jnp.where(here, jnp.maximum(found, top), found)
                else:
                    values = jnp.exp(scores + target_pot[step, slot_at(row, slot)])
                    found = found + jnp.where(here, jnp.sum(values, axis=0, keepdims=True), 0.0)
        return found

    def column_result(best):
        best_rows[...] = best.reshape(GB, 1, BLK)
        every = [(row, slot) for row in range(ROWS) for slot in range(SLOTS)]
        tops = jnp.concatenate([best_rows[slot_at(row, slot)] for row, slot in every], axis=0)
        values = sums[...] * jnp.exp(peaks[...] - tops)
        total = jnp.zeros((GB, BLK), f32)
        for block, (row, slot) in enumerate(every):
            total = total + jnp.where(position == slot_at(row, slot), values[block : block + 1, :], 0.0)
        return jnp.where(total > 0.0, best + jnp.log(jnp.maximum(total, 1e-30)), LOW)

    def exchange(step, pieces):
        copies = []
        for number in FARTHEST_FIRST:
            src, dst = pieces(number)
            send_at, recv_at = merge_send.at[step, number], merge_recv.at[step, number]
            copies.append(remote(src, dst, send_at, recv_at, device(number // 4, number % 4)))
            start(copies[-1])
        for copy in copies:
            copy.wait_recv()

    def iteration(step):
        if step:

            def row_body(part, _):
                row_pass(step, part)
                return 0

            lax.fori_loop(0, PARTS, row_body, 0)
        combine = add_up if step else merge
        found = jnp.full((GB, BLK), 0.0 if step else LOW, f32)
        found = lax.fori_loop(0, PARTS, functools.partial(column_part, step), found)
        half_out[step] = found if step else column_result(found)
        copy = remote(
            half_out.at[step, other_half], half_land.at[step], half_send.at[step], half_recv.at[step], device(0, 0, 1)
        )
        start(copy)
        copy.wait_recv()
        merged[step] = combine([half_out[step, half, :], half_land[step]])
        if step < ITERS - 1:
            exchange(step, lambda number: (merged.at[step], merged_land.at[step, number - 1]))
            total = combine([merged[step]] + [merged_land[step, n] for n in range(15)])
            if step:
                own = target_pot[step, half].reshape(16, BLK) + (log_target[half, :] - jnp.log(total))
            else:
                own = log_target[half, :] - total
            here = target_pot.at[step + 1, half]
            here[...] = own.reshape(16, 1, BLK)
            copy = remote(here, here, pot_send.at[step], pot_recv.at[step], device(0, 0, 1))
            start(copy)
            copy.wait_recv()
        else:
            def pieces(number):
                theirs_at = ((z + number // 4) % 4) * 4 + (y + number % 4) % 4
                return merged.at[step, pl.ds(theirs_at, 1)], merged_land.at[step, number - 1, pl.ds(0, 1)]

            exchange(step, pieces)
            own = z * 4 + y
            total = combine([merged[step, pl.ds(own, 1), :]] + [merged_land[step, n, 0:1, :] for n in range(15)])
            change = log_target[pl.ds(mine + own, 1), :] - jnp.log(total)
            target_out[...] = (target_pot[step, mine + own] + change) * ENTROPY

    for step in range(ITERS):
        iteration(step)
    for step, part, dx in itertools.product(range(ITERS), range(PARTS), (1, 2, 3)):
        row_copy(step, part, dx).wait_send()
    source_out[...] = source_pot[...] * ENTROPY
    for copy in started:
        copy.wait_send()
    out_copy.wait()


def hand_over(cost, source, target, cost_out, source_out, target_out, held, source_held, target_held, load, store):
    parts = 4
    size = held.shape[0] // parts
    rows = [pl.ds(n * size, size) for n in range(parts)]
    steps = [(cost.at[r], held.at[r], cost_out.at[r]) for r in rows]
    steps[1:1] = [(source, source_held, source_out), (target, target_held, target_out)]
    loads = [pltpu.make_async_copy(src, here, load.at[n]) for n, (src, here, _) in enumerate(steps)]
    stores = [pltpu.make_async_copy(here, dst, store.at[n]) for n, (_, here, dst) in enumerate(steps)]
    for copy in loads:
        copy.start()
    for came, goes in zip(loads, stores):
        came.wait()
        goes.start()
    for copy in stores:
        copy.wait()


def per_device(
    coupling,
    coupling_index,
    near_cost,
    near_index,
    source_weights,
    target_cost,
    target_index,
    target_weights,
):
    vmem = pl.BlockSpec(memory_space=pltpu.VMEM)
    anywhere = pl.BlockSpec(memory_space=pl.ANY)
    dma = pltpu.SemaphoreType.DMA
    moves = len(NUMBER)
    blocks = ROWS * SLOTS
    cost, source, target = pl.pallas_call(
        kernel,
        out_shape=(
            jax.ShapeDtypeStruct((blocks, BLK, BLK), f32),
            jax.ShapeDtypeStruct((ROWS, BLK), f32),
            jax.ShapeDtypeStruct((1, BLK), f32),
        ),
        in_specs=[anywhere] * 8,
        out_specs=(anywhere, vmem, vmem),
        scratch_shapes=[
            pltpu.SMEM((SLOTS, ROWS), jnp.int32),
            pltpu.SMEM((NEAR, ROWS), jnp.int32),
            pltpu.SMEM((LINKS, 1, GB), jnp.int32),
            pltpu.VMEM((ROWS, BLK), jnp.int32),
            pltpu.VMEM((1, BLK), jnp.int32),
            pltpu.VMEM((ROWS * NEAR, BLK, BLK), f32),
            pltpu.VMEM((blocks, BLK, BLK), f32),
            pltpu.VMEM((ROWS, BLK, 2 * BLK), bf16),
            pltpu.VMEM((ROWS, BLK, 2 * BLK), bf16),
            pltpu.VMEM((ROWS, 2 * BLK, 6 * BLK), bf16),
            pltpu.VMEM((ROWS, BLK, BLK), f32),
            pltpu.VMEM((GB * SHARD, BLK), f32),
            pltpu.VMEM((GB * LINKS + 1, BLK, BLK), bf16),
            pltpu.VMEM((GB * LINKS + 1, BLK, BLK), bf16),
            pltpu.VMEM((blocks, BLK, BLK), f32),
            pltpu.VMEM((ROWS, BLK), f32),
            pltpu.VMEM((ROWS, 1, BLK), f32),
            pltpu.VMEM((1, BLK), f32),
            pltpu.VMEM((4, 1, BLK), f32),
            pltpu.VMEM((2, 4, 4, 8, BLK), f32),
            pltpu.VMEM((GB, 1, BLK), f32),
            pltpu.VMEM((ROWS, BLK), f32),
            pltpu.VMEM((GB, BLK), f32),
            pltpu.VMEM((ITERS, ROWS, BLK), f32),
            pltpu.VMEM((ITERS, 3, ROWS, BLK), f32),
            pltpu.VMEM((ROWS, BLK), f32),
            pltpu.VMEM((ITERS, GB, BLK), f32),
            pltpu.VMEM((ITERS, 16, BLK), f32),
            pltpu.VMEM((ITERS, 16, BLK), f32),
            pltpu.VMEM((ITERS, 15, 16, BLK), f32),
            pltpu.VMEM((ITERS + 1, GB, 1, BLK), f32),
            pltpu.VMEM((blocks, BLK), f32),
            pltpu.VMEM((blocks, BLK), f32),
            pltpu.VMEM((GB, 1, BLK), f32),
            dma((15,)),
            dma((moves,)),
            dma((moves,)),
            dma((moves + 1,)),
            dma((moves + 1,)),
            dma((4,)),
            dma((4,)),
            dma((7,)),
            dma((7,)),
            dma((ITERS, PARTS, 4)),
            dma((ITERS, PARTS, 4)),
            dma((ITERS,)),
            dma((ITERS,)),
            dma((ITERS, 16)),
            dma((ITERS, 16)),
            dma((ITERS,)),
            dma((ITERS,)),
        ],
        compiler_params=pltpu.CompilerParams(
            collective_id=0, has_side_effects=True, vmem_limit_bytes=60 * 2**20
        ),
        name="gromov_step",
    )(
        coupling_index.transpose(1, 2, 0).reshape(SLOTS, ROWS),
        near_index.T,
        target_index.transpose(2, 0, 1),
        source_weights.reshape(ROWS, BLK),
        target_weights,
        coupling.reshape(blocks, BLK, BLK),
        near_cost.reshape(ROWS * NEAR, BLK, BLK),
        target_cost.reshape(SHARD, BLK),
    )
    cost, source, target = pl.pallas_call(
        hand_over,
        out_shape=tuple(jax.ShapeDtypeStruct(x.shape, x.dtype) for x in (cost, source, target)),
        in_specs=[anywhere] * 3,
        out_specs=(anywhere,) * 3,
        scratch_shapes=[
            pltpu.VMEM((blocks, BLK, BLK), f32),
            pltpu.VMEM((ROWS, BLK), f32),
            pltpu.VMEM((1, BLK), f32),
            dma((6,)),
            dma((6,)),
        ],
        compiler_params=pltpu.CompilerParams(vmem_limit_bytes=60 * 2**20),
        name="hand_over",
    )(cost, source, target)
    return (
        cost.reshape(ROWS, 1, SLOTS, BLK, BLK),
        source.reshape(ROWS * BLK),
        target,
    )


def solution(mesh):
    placed = (
        P("rows", "cols", None, None, None),
        P("rows", "cols", None),
        P("rows", None, None, None),
        P("rows", None),
        P("rows"),
        P("cols", "rows", None, None, None),
        P("cols", None, None),
        P("cols", "rows"),
    )
    return jax.shard_map(
        per_device,
        mesh=mesh,
        in_specs=placed,
        out_specs=(P("rows", "cols", None, None, None), P("rows"), P("cols", "rows")),
        check_vma=False,
    )
```

```python
import functools
import itertools

import jax
import jax.numpy as jnp
from jax import lax
from jax.experimental import pallas as pl
from jax.experimental.pallas import tpu as pltpu
from jax.sharding import PartitionSpec as P

MESH = pl.DeviceIdType.MESH
BLK = 128
ROWS = 32
NEAR = 3
LINKS = 3
SLOTS = 2
GB = 32
ITERS = 3
SHARD = LINKS * BLK
HALF = SHARD // 2
QUARTER = SHARD // 4
COLS = 4
ENTROPY = 0.01
LOW = -1e30
f32 = jnp.float32
bf16 = jnp.bfloat16


def gather_plan():
    pieces = []
    for half, dz, dy, part in itertools.product(range(2), range(4), range(4), range(2)):
        if dz == 0 and dy == 0:
            continue
        first_axis = dy if half == 0 else dz
        last_axis = dz if half == 0 else dy
        axis = ("z" if half == 0 else "y") if last_axis else ("y" if half == 0 else "z")
        far = last_axis if last_axis else first_axis
        side = {1: 1, 3: -1, 2: 2 * part - 1}[far]
        came = ((dz - side) % 4, dy) if axis == "z" else (dz, (dy - side) % 4)
        pieces.append((half, dz, dy, part, axis, side, came))

    def onward(piece):
        half, dz, dy, part = piece[:4]
        after = [p for p in pieces if p[0] == half and p[3] == part and p[6] == (dz, dy)]
        return max([1 + onward(p) for p in after], default=0)

    hops = {p: onward(p) for p in pieces}
    have = {(half, 0, 0, part): 0 for half in range(2) for part in range(2)}
    left = list(pieces)
    sends = []
    arrivals = []
    slot = 0
    while left:
        sends.append([])
        for link in itertools.product("yz", (1, -1)):
            ready = [
                p
                for p in left
                if (p[4], p[5]) == link and have.get((p[0],) + p[6] + (p[3],), slot + 1) <= slot
            ]
            if ready:
                best = max(ready, key=lambda p: (hops[p], -have[(p[0],) + p[6] + (p[3],)], -left.index(p)))
                left.remove(best)
                sends[-1].append(best)
                have[best[:4]] = slot + 1 + DELAY
                arrivals.append(best)
        slot += 1
    arrivals.sort(key=lambda p: have[p[:4]])
    takes = [[p for p in arrivals if have[p[:4]] == when] for when in range(slot + 1 + DELAY)]
    number = {p: n for n, p in enumerate(arrivals)}
    return number, sends, takes


DELAY = 3
PARTS = 2
FARTHEST_FIRST = sorted(range(1, 16), key=lambda n: abs(n // 4 - 2) + abs(n % 4 - 2))
NUMBER, SENDS, TAKES = gather_plan()


def split(value):
    high = value.astype(bf16)
    return high, (value - high.astype(f32)).astype(bf16)


def dot(a, b):
    return jnp.dot(a, b, preferred_element_type=f32)


def kernel(
    slots_hbm,
    near_index_hbm,
    links_hbm,
    source_hbm,
    weight_hbm,
    coupling_hbm,
    near_hbm,
    target_hbm,
    cost_hbm,
    source_out,
    target_out,
    slots,
    near,
    links,
    source_ref,
    weight_ref,
    near_cost,
    plan,
    plan_high,
    plan_low,
    partial,
    row_sum,
    gathered,
    far_high,
    far_low,
    shifted,
    source_float,
    source_rows,
    weight_float,
    weight_land,
    extra,
    column,
    log_source,
    log_target,
    row_lse,
    row_land,
    source_pot,
    half_out,
    half_land,
    merged,
    merged_land,
    target_pot,
    peaks,
    sums,
    best_rows,
    load_sem,
    gather_send,
    gather_recv,
    pair_send,
    pair_recv,
    early_send,
    early_recv,
    extra_send,
    extra_recv,
    row_send,
    row_recv,
    half_send,
    half_recv,
    merge_send,
    merge_recv,
    pot_send,
    pot_recv,
):
    cost = plan
    scaled = near_cost

    rank = lax.axis_index("rows")
    group = lax.axis_index("cols")
    z = rank // 8
    y = (rank // 2) % 4
    core = rank % 2

    def at(dz, dy, other=0):
        return (((z + dz) % 4) * 4 + (y + dy) % 4) * 2 + (core + other) % 2

    def device(dz, dy, other=0, dx=0):
        return (at(dz, dy, other), (group + dx) % COLS)

    def remote(src, dst, send, recv, where):
        return pltpu.make_async_remote_copy(
            src_ref=src, dst_ref=dst, send_sem=send, recv_sem=recv, device_id=where, device_id_type=MESH
        )

    def piece_rows(dz, dy, half, part, other=0):
        first = at(dz, dy, other) * SHARD + half * HALF + part * QUARTER
        return gathered.at[pl.ds(pl.multiple_of(first, 8), QUARTER)]

    loads = []
    chunk = ROWS // 4
    for part in range(4):
        loads.append(
            pltpu.make_async_copy(
                coupling_hbm.at[pl.ds(part * chunk * SLOTS, chunk * SLOTS)],
                plan.at[pl.ds(part * chunk * SLOTS, chunk * SLOTS)],
                load_sem.at[part],
            )
        )
    for part in range(4):
        loads.append(
            pltpu.make_async_copy(
                near_hbm.at[pl.ds(part * chunk * NEAR, chunk * NEAR)],
                near_cost.at[pl.ds(part * chunk * NEAR, chunk * NEAR)],
                load_sem.at[4 + part],
            )
        )
    small = []
    for number, (src, dst) in enumerate(
        [
            (weight_hbm, weight_ref),
            (source_hbm, source_ref),
            (near_index_hbm, near),
            (slots_hbm, slots),
            (links_hbm, links),
        ]
    ):
        small.append(pltpu.make_async_copy(src, dst, load_sem.at[10 + number]))
    own_rows = gathered.at[pl.ds(pl.multiple_of(rank * SHARD, 8), SHARD)]
    own_load = pltpu.make_async_copy(target_hbm, own_rows, load_sem.at[8])

    barrier = pltpu.get_barrier_semaphore()
    neighbours = [device(0, 0, 1), device(0, 1), device(0, 3), device(1, 0), device(3, 0)]
    neighbours += [device(0, 0, 0, dx) for dx in (1, 3)]
    for where in neighbours:
        pl.semaphore_signal(barrier, inc=1, device_id=where, device_id_type=MESH)
    for copy in small + [own_load] + loads:
        copy.start()
    small[0].wait()
    weight_float[...] = weight_ref[...].astype(f32)
    pl.semaphore_wait(barrier, len(neighbours))

    started = []

    def start(copy):
        copy.start()
        started.append(copy)

    def send(piece):
        half, dz, dy, part, axis, side, came = piece
        dst = piece_rows(*came, half, part)
        if came == (0, 0):
            src = target_hbm.at[pl.ds(half * HALF + part * QUARTER, QUARTER)]
        else:
            src = dst
        number = NUMBER[piece]
        where = device(-side, 0) if axis == "z" else device(0, -side)
        start(remote(src, dst, gather_send.at[number], gather_recv.at[number], where))

    def split_rows(owner, half, part):
        first = half * HALF + part * QUARTER
        end = first + QUARTER
        while first < end:
            link = first // BLK
            size = min(end, (link + 1) * BLK) - first
            high, low = split(gathered[pl.ds(pl.multiple_of(owner * SHARD + first, 8), size), :])
            far_high[owner * LINKS + link, first - link * BLK : first - link * BLK + size, :] = high
            far_low[owner * LINKS + link, first - link * BLK : first - link * BLK + size, :] = low
            first += size

    def pair_copy(piece, other):
        here = piece_rows(piece[1], piece[2], piece[0], piece[3], other)
        number = NUMBER[piece]
        return remote(here, here, pair_send.at[number], pair_recv.at[number], device(0, 0, 1))

    def take(slot):
        pieces = TAKES[slot] if slot < len(TAKES) else []
        for piece in pieces:
            half, dz, dy, part = piece[:4]
            here = piece_rows(dz, dy, half, part)
            number = NUMBER[piece]
            remote(here, here, gather_send.at[number], gather_recv.at[number], device(0, 0, 1)).wait_recv()
            start(pair_copy(piece, 0))
        return pieces

    def use(pieces, other):
        for piece in pieces:
            if other:
                pair_copy(piece, 1).wait_recv()
            split_rows(at(piece[1], piece[2], other), piece[0], piece[3])

    def slot_at(row, slot):
        wanted = slots[slot, row]
        return lax.rem(wanted, 2) * 16 + lax.div(wanted, 2)

    def block_at(far, wanted):
        found = jnp.int32(GB * LINKS)
        for link in range(LINKS):
            found = jnp.where(links[link, 0, far] == wanted, far * LINKS + link, found)
        return found

    def split_plan(row, _):
        for q in range(SLOTS):
            high, low = split(plan[row * SLOTS + q])
            plan_high[row, :, q * BLK : (q + 1) * BLK] = high
            plan_low[row, :, q * BLK : (q + 1) * BLK] = low
        return 0

    def first_product(pair, _):
        for row in (2 * pair, 2 * pair + 1):
            total = jnp.zeros((BLK, BLK), f32)
            for k in range(NEAR):
                other = lax.rem(near[k, row], ROWS)
                block = near_cost[row * NEAR + k]
                high, low = split(block)
                high_plan = plan_high[other]
                low_plan = plan_low[other]
                both = jnp.concatenate([high, low], axis=1)
                result = dot(both, jnp.concatenate([high_plan, high_plan], axis=0)) + dot(high, low_plan)
                result_high, result_low = split(result)
                partial[row, 0:BLK, k * 2 * BLK : (k + 1) * 2 * BLK] = result_high
                partial[row, BLK : 2 * BLK, k * 2 * BLK : (k + 1) * 2 * BLK] = result_low
                total = total + block * block * source_rows[other]
            row_sum[row] = jnp.broadcast_to(jnp.sum(total, axis=1, keepdims=True), (BLK, BLK))
        return 0

    def first_rows(low, high):
        for part in range(4):
            if low <= part * chunk < high:
                loads[4 + part].wait()
        lax.fori_loop(low // 2, high // 2, first_product, 0)

    def plan_rows(part):
        loads[part].wait()
        lax.fori_loop(part * chunk, (part + 1) * chunk, split_plan, 0)

    def own_share():
        own_load.wait()
        own_weight = weight_float[...]
        weight_column = jnp.broadcast_to(own_weight, (BLK, BLK)).T
        extra_rows = [own_weight]
        for link in range(LINKS):
            block = gathered[pl.ds(pl.multiple_of(rank * SHARD + link * BLK, 8), BLK), :]
            extra_rows.append(jnp.sum(block * block * weight_column, axis=0, keepdims=True))
        across = own_weight
        for dx in (3, 2):
            early(dx).wait_recv()
        for dx in (1, 2, 3):
            across = across + weight_land[dx]
        extra_rows.append(across)
        extra_rows.append(jnp.sum(source_float[...], axis=0, keepdims=True))
        extra_rows.append(jnp.zeros((2, BLK), f32))
        extra[core, z, y] = jnp.concatenate(extra_rows, axis=0)

    def early(dx):
        src = weight_land.at[1] if dx == 2 else weight_float
        where = device(0, 0, 0, 1 if dx == 2 else dx)
        return remote(src, weight_land.at[dx], early_send.at[dx], early_recv.at[dx], where)

    def extra_copy(number):
        if number == 0:
            here, where = extra.at[core], device(0, 0, 1)
        elif number < 4:
            here, where = extra.at[core, z, y], device(0, number)
        else:
            here, where = extra.at[core, z], device(number - 3, 0)
        return remote(here, here, extra_send.at[number], extra_recv.at[number], where)

    position = lax.broadcasted_iota(jnp.int32, (GB, BLK), 0)
    row_scale_at = []

    def masses():
        everything = extra[...].reshape(GB, 8, BLK)
        target_total = jnp.sum(everything[:, 4, :])
        source_total = jnp.sum(everything[:, 5, :])
        target_scale = (COLS * GB * BLK) / target_total
        source_scale = (GB * ROWS * BLK) / source_total
        log_source[...] = jnp.log(source_float[...] * source_scale)
        log_target[...] = jnp.log(everything[:, 0, :] * target_scale)
        column_scale = target_scale / (LINKS * BLK)
        row_scale = source_scale / (NEAR * BLK)

        def add_column(step, total):
            own = (step % 16) * 2 + step // 16
            for link in range(LINKS):
                lands = links[link, 0, own]
                lands = lax.rem(lands, 2) * 16 + lax.div(lands, 2)
                value = extra[step // 16, (step // 4) % 4, step % 4, 1 + link : 2 + link, :]
                total = total + jnp.where(position == lands, value, 0.0)
            return total

        column_term = lax.fori_loop(0, GB, add_column, jnp.zeros((GB, BLK), f32), unroll=4) * column_scale
        column[...] = column_term.reshape(GB, 1, BLK)
        row_scale_at.append(row_scale)

    pair_own = len(NUMBER)
    from_pair = []
    rows_done = 0
    for slot in range(len(TAKES) + 2):
        taken = take(slot)
        if slot < len(SENDS):
            for piece in SENDS[slot]:
                send(piece)
        if slot == 0:
            plan_rows(0)
            plan_rows(1)
            for copy in small[1:]:
                copy.wait()
            source_float[...] = source_ref[...].astype(f32)
            source_rows[...] = source_float[...].reshape(ROWS, 1, BLK)
        elif slot == 1:
            plan_rows(2)
            plan_rows(3)
            own_rows = gathered.at[pl.ds(pl.multiple_of(rank * SHARD, 8), SHARD)]
            start(remote(target_hbm, own_rows, pair_send.at[pair_own], pair_recv.at[pair_own], device(0, 0, 1)))
            start(early(1))
            start(early(3))
        elif slot == 4:
            early(1).wait_recv()
            start(early(2))
        elif slot == 6:
            own_share()
            for half, part in itertools.product(range(2), range(2)):
                split_rows(rank, half, part)
        elif slot == 8:
            for number in (1, 2, 3):
                start(extra_copy(number))
        elif slot == 11:
            for number in (1, 2, 3):
                extra_copy(number).wait_recv()
            for number in (4, 5, 6):
                start(extra_copy(number))
        elif slot == 15:
            for number in (4, 5, 6):
                extra_copy(number).wait_recv()
            start(extra_copy(0))
        use(taken, 0)
        from_pair.append(taken)
        if slot >= 2:
            use(from_pair[slot - 2], 1)
        if slot >= 2 and rows_done < ROWS:
            more = min(ROWS, rows_done + 4)
            first_rows(rows_done, more)
            rows_done = more
    here = gathered.at[pl.ds(pl.multiple_of(at(0, 0, 1) * SHARD, 8), SHARD)]
    remote(here, here, pair_send.at[pair_own], pair_recv.at[pair_own], device(0, 0, 1)).wait_recv()
    for half, part in itertools.product(range(2), range(2)):
        split_rows(at(0, 0, 1), half, part)
    extra_copy(0).wait_recv()
    masses()
    far_high[GB * LINKS] = jnp.zeros((BLK, BLK), bf16)
    far_low[GB * LINKS] = jnp.zeros((BLK, BLK), bf16)

    factor = 2.0 / (NEAR * BLK) / (COLS * SLOTS * BLK)

    def second_row(row):
        high_rows = []
        low_rows = []
        wanted = [slots[slot, row] for slot in range(SLOTS)]
        for k in range(NEAR):
            other = lax.rem(near[k, row], ROWS)
            for q in range(SLOTS):
                far = slots[q, other]
                found = [block_at(far, wanted[slot]) for slot in range(SLOTS)]
                high_rows.append(jnp.concatenate([far_high[n] for n in found], axis=1))
                low_rows.append(jnp.concatenate([far_low[n] for n in found], axis=1))
        result = dot(partial[row], jnp.concatenate(high_rows, axis=0))
        result = result[0:BLK] + result[BLK : 2 * BLK]
        result = result + dot(partial[row, 0:BLK, :], jnp.concatenate(low_rows, axis=0))
        across = row_sum[row] * row_scale_at[0]
        scores = []
        for slot in range(SLOTS):
            own_column = column[slot_at(row, slot)]
            value = across + own_column - factor * result[:, slot * BLK : (slot + 1) * BLK]
            cost[row * SLOTS + slot] = value
            value = value * (1.0 / ENTROPY)
            scaled[row * SLOTS + slot] = value
            scores.append(-value)
        return scores

    def row_sums(scores):
        top = jnp.max(jnp.maximum(scores[0], scores[1]), axis=1, keepdims=True)
        total = jnp.sum(jnp.exp(scores[0] - top) + jnp.exp(scores[1] - top), axis=1, keepdims=True)
        return top, total

    def row_result(found):
        tops = jnp.concatenate([top for top, _ in found], axis=1).T
        totals = jnp.concatenate([total for _, total in found], axis=1).T
        return tops + jnp.log(totals)

    part_rows = ROWS // PARTS

    def row_copy(step, part, dx):
        rows = pl.ds(pl.multiple_of(part * part_rows, part_rows), part_rows)
        return remote(
            row_lse.at[step, rows],
            row_land.at[step, dx - 1, rows],
            row_send.at[step, part, dx],
            row_recv.at[step, part, dx],
            device(0, 0, 0, dx),
        )

    def send_rows(step, part, value):
        row_lse[step, pl.ds(pl.multiple_of(part * part_rows, part_rows), part_rows), :] = value
        for dx in (2, 1, 3):
            row_copy(step, part, dx).start()

    def second_product(part, _):
        found = [row_sums(second_row(part * part_rows + inner)) for inner in range(part_rows)]
        send_rows(0, part, row_result(found))
        return 0

    lax.fori_loop(0, PARTS, second_product, 0)
    out_copy = pltpu.make_async_copy(cost, cost_hbm, load_sem.at[9])
    out_copy.start()

    mine = core * 16
    theirs = 16 - mine
    half = pl.ds(pl.multiple_of(mine, 16), 16)
    other_half = pl.ds(pl.multiple_of(theirs, 16), 16)

    def row_pass(step, part):
        totals = []
        for inner in range(part_rows):
            row = part * part_rows + inner
            values = [
                jnp.exp(shifted[row * SLOTS + slot] + target_pot[step, slot_at(row, slot)]) for slot in range(SLOTS)
            ]
            totals.append(jnp.sum(values[0] + values[1], axis=1, keepdims=True))
        send_rows(step, part, jnp.concatenate(totals, axis=1).T)

    def merge(values):
        top = functools.reduce(jnp.maximum, values)
        total = functools.reduce(jnp.add, [jnp.exp(value - top) for value in values])
        return top + jnp.log(total)

    def add_up(values):
        return functools.reduce(jnp.add, values)

    def column_part(step, part, found):
        for dx in (1, 3, 2):
            row_copy(step, part, dx).wait_recv()
        rows = pl.ds(pl.multiple_of(part * part_rows, part_rows), part_rows)
        arrived = [row_lse[step, rows, :]] + [row_land[step, n, rows, :] for n in range(3)]
        if step == 0:
            potentials = log_source[rows, :] - merge(arrived)
        else:
            potentials = source_pot[rows, :] + (log_source[rows, :] - jnp.log(add_up(arrived)))
        source_pot[rows, :] = potentials
        potentials = potentials.T
        for inner in range(part_rows):
            row = part * part_rows + inner
            potential = potentials[:, inner : inner + 1]
            for slot in range(SLOTS):
                block = row * SLOTS + slot
                here = position == slot_at(row, slot)
                scores = potential - scaled[block]
                if step < ITERS - 1:
                    shifted[block] = scores
                if step == 0:
                    top = jnp.max(scores, axis=0, keepdims=True)
                    total = jnp.sum(jnp.exp(scores - top), axis=0, keepdims=True)
                    peaks[pl.ds(block, 1), :] = top
                    sums[pl.ds(block, 1), :] = total
                    found = jnp.where(here, jnp.maximum(found, top), found)
                else:
                    values = jnp.exp(scores + target_pot[step, slot_at(row, slot)])
                    found = found + jnp.where(here, jnp.sum(values, axis=0, keepdims=True), 0.0)
        return found

    def column_result(best):
        best_rows[...] = best.reshape(GB, 1, BLK)
        every = [(row, slot) for row in range(ROWS) for slot in range(SLOTS)]
        tops = jnp.concatenate([best_rows[slot_at(row, slot)] for row, slot in every], axis=0)
        values = sums[...] * jnp.exp(peaks[...] - tops)
        total = jnp.zeros((GB, BLK), f32)
        for block, (row, slot) in enumerate(every):
            total = total + jnp.where(position == slot_at(row, slot), values[block : block + 1, :], 0.0)
        return jnp.where(total > 0.0, best + jnp.log(jnp.maximum(total, 1e-30)), LOW)

    def exchange(step, pieces):
        copies = []
        for number in FARTHEST_FIRST:
            src, dst = pieces(number)
            send_at, recv_at = merge_send.at[step, number], merge_recv.at[step, number]
            copies.append(remote(src, dst, send_at, recv_at, device(number // 4, number % 4)))
            start(copies[-1])
        for copy in copies:
            copy.wait_recv()

    def iteration(step):
        if step:

            def row_body(part, _):
                row_pass(step, part)
                return 0

            lax.fori_loop(0, PARTS, row_body, 0)
        combine = add_up if step else merge
        found = jnp.full((GB, BLK), 0.0 if step else LOW, f32)
        found = lax.fori_loop(0, PARTS, functools.partial(column_part, step), found)
        half_out[step] = found if step else column_result(found)
        copy = remote(
            half_out.at[step, other_half], half_land.at[step], half_send.at[step], half_recv.at[step], device(0, 0, 1)
        )
        start(copy)
        copy.wait_recv()
        merged[step] = combine([half_out[step, half, :], half_land[step]])
        if step < ITERS - 1:
            exchange(step, lambda number: (merged.at[step], merged_land.at[step, number - 1]))
            total = combine([merged[step]] + [merged_land[step, n] for n in range(15)])
            if step:
                own = target_pot[step, half].reshape(16, BLK) + (log_target[half, :] - jnp.log(total))
            else:
                own = log_target[half, :] - total
            here = target_pot.at[step + 1, half]
            here[...] = own.reshape(16, 1, BLK)
            copy = remote(here, here, pot_send.at[step], pot_recv.at[step], device(0, 0, 1))
            start(copy)
            copy.wait_recv()
        else:
            def pieces(number):
                theirs_at = ((z + number // 4) % 4) * 4 + (y + number % 4) % 4
                return merged.at[step, pl.ds(theirs_at, 1)], merged_land.at[step, number - 1, pl.ds(0, 1)]

            exchange(step, pieces)
            own = z * 4 + y
            total = combine([merged[step, pl.ds(own, 1), :]] + [merged_land[step, n, 0:1, :] for n in range(15)])
            change = log_target[pl.ds(mine + own, 1), :] - jnp.log(total)
            target_out[...] = (target_pot[step, mine + own] + change) * ENTROPY

    for step in range(ITERS):
        iteration(step)
    for step, part, dx in itertools.product(range(ITERS), range(PARTS), (1, 2, 3)):
        row_copy(step, part, dx).wait_send()
    source_out[...] = source_pot[...] * ENTROPY
    for copy in started:
        copy.wait_send()
    out_copy.wait()


def hand_over(cost, source, target, cost_out, source_out, target_out, held, source_held, target_held, load, store):
    parts = 4
    size = held.shape[0] // parts
    rows = [pl.ds(n * size, size) for n in range(parts)]
    steps = [(cost.at[r], held.at[r], cost_out.at[r]) for r in rows]
    steps[1:1] = [(source, source_held, source_out), (target, target_held, target_out)]
    loads = [pltpu.make_async_copy(src, here, load.at[n]) for n, (src, here, _) in enumerate(steps)]
    stores = [pltpu.make_async_copy(here, dst, store.at[n]) for n, (_, here, dst) in enumerate(steps)]
    for copy in loads:
        copy.start()
    for came, goes in zip(loads, stores):
        came.wait()
        goes.start()
    for copy in stores:
        copy.wait()


def per_device(
    coupling,
    coupling_index,
    near_cost,
    near_index,
    source_weights,
    target_cost,
    target_index,
    target_weights,
):
    vmem = pl.BlockSpec(memory_space=pltpu.VMEM)
    anywhere = pl.BlockSpec(memory_space=pl.ANY)
    dma = pltpu.SemaphoreType.DMA
    moves = len(NUMBER)
    blocks = ROWS * SLOTS
    cost, source, target = pl.pallas_call(
        kernel,
        out_shape=(
            jax.ShapeDtypeStruct((blocks, BLK, BLK), f32),
            jax.ShapeDtypeStruct((ROWS, BLK), f32),
            jax.ShapeDtypeStruct((1, BLK), f32),
        ),
        in_specs=[anywhere] * 8,
        out_specs=(anywhere, vmem, vmem),
        scratch_shapes=[
            pltpu.SMEM((SLOTS, ROWS), jnp.int32),
            pltpu.SMEM((NEAR, ROWS), jnp.int32),
            pltpu.SMEM((LINKS, 1, GB), jnp.int32),
            pltpu.VMEM((ROWS, BLK), jnp.int32),
            pltpu.VMEM((1, BLK), jnp.int32),
            pltpu.VMEM((ROWS * NEAR, BLK, BLK), f32),
            pltpu.VMEM((blocks, BLK, BLK), f32),
            pltpu.VMEM((ROWS, BLK, 2 * BLK), bf16),
            pltpu.VMEM((ROWS, BLK, 2 * BLK), bf16),
            pltpu.VMEM((ROWS, 2 * BLK, 6 * BLK), bf16),
            pltpu.VMEM((ROWS, BLK, BLK), f32),
            pltpu.VMEM((GB * SHARD, BLK), f32),
            pltpu.VMEM((GB * LINKS + 1, BLK, BLK), bf16),
            pltpu.VMEM((GB * LINKS + 1, BLK, BLK), bf16),
            pltpu.VMEM((blocks, BLK, BLK), f32),
            pltpu.VMEM((ROWS, BLK), f32),
            pltpu.VMEM((ROWS, 1, BLK), f32),
            pltpu.VMEM((1, BLK), f32),
            pltpu.VMEM((4, 1, BLK), f32),
            pltpu.VMEM((2, 4, 4, 8, BLK), f32),
            pltpu.VMEM((GB, 1, BLK), f32),
            pltpu.VMEM((ROWS, BLK), f32),
            pltpu.VMEM((GB, BLK), f32),
            pltpu.VMEM((ITERS, ROWS, BLK), f32),
            pltpu.VMEM((ITERS, 3, ROWS, BLK), f32),
            pltpu.VMEM((ROWS, BLK), f32),
            pltpu.VMEM((ITERS, GB, BLK), f32),
            pltpu.VMEM((ITERS, 16, BLK), f32),
            pltpu.VMEM((ITERS, 16, BLK), f32),
            pltpu.VMEM((ITERS, 15, 16, BLK), f32),
            pltpu.VMEM((ITERS + 1, GB, 1, BLK), f32),
            pltpu.VMEM((blocks, BLK), f32),
            pltpu.VMEM((blocks, BLK), f32),
            pltpu.VMEM((GB, 1, BLK), f32),
            dma((15,)),
            dma((moves,)),
            dma((moves,)),
            dma((moves + 1,)),
            dma((moves + 1,)),
            dma((4,)),
            dma((4,)),
            dma((7,)),
            dma((7,)),
            dma((ITERS, PARTS, 4)),
            dma((ITERS, PARTS, 4)),
            dma((ITERS,)),
            dma((ITERS,)),
            dma((ITERS, 16)),
            dma((ITERS, 16)),
            dma((ITERS,)),
            dma((ITERS,)),
        ],
        compiler_params=pltpu.CompilerParams(
            collective_id=0, has_side_effects=True, vmem_limit_bytes=60 * 2**20
        ),
        name="gromov_step",
    )(
        coupling_index.transpose(1, 2, 0).reshape(SLOTS, ROWS),
        near_index.T,
        target_index.transpose(2, 0, 1),
        source_weights.reshape(ROWS, BLK),
        target_weights,
        coupling.reshape(blocks, BLK, BLK),
        near_cost.reshape(ROWS * NEAR, BLK, BLK),
        target_cost.reshape(SHARD, BLK),
    )
    cost, source, target = pl.pallas_call(
        hand_over,
        out_shape=tuple(jax.ShapeDtypeStruct(x.shape, x.dtype) for x in (cost, source, target)),
        in_specs=[anywhere] * 3,
        out_specs=(anywhere,) * 3,
        scratch_shapes=[
            pltpu.VMEM((blocks, BLK, BLK), f32),
            pltpu.VMEM((ROWS, BLK), f32),
            pltpu.VMEM((1, BLK), f32),
            dma((6,)),
            dma((6,)),
        ],
        compiler_params=pltpu.CompilerParams(vmem_limit_bytes=60 * 2**20),
        name="hand_over",
    )(cost, source, target)
    return (
        cost.reshape(ROWS, 1, SLOTS, BLK, BLK),
        source.reshape(ROWS * BLK),
        target,
    )


def solution(mesh):
    placed = (
        P("rows", "cols", None, None, None),
        P("rows", "cols", None),
        P("rows", None, None, None),
        P("rows", None),
        P("rows"),
        P("cols", "rows", None, None, None),
        P("cols", None, None),
        P("cols", "rows"),
    )
    return jax.shard_map(
        per_device,
        mesh=mesh,
        in_specs=placed,
        out_specs=(P("rows", "cols", None, None, None), P("rows"), P("cols", "rows")),
        check_vma=False,
    )
```
